32 devices in a mesh: ctx: 8 (over z, x), tp: 4 (over y, core).
Axes of the slice: x: 2, y: 2, z: 4, core: 2. Of those that a mesh axis runs over, the one named last changes fastest.
Arguments:
- tokens: bfloat16 [4096, 4096], P('ctx', 'tp'), may hold values from -16 to 16
- query_weight: bfloat16 [4096, 4096], P(None, 'tp'), may hold values from -0.09375 to 0.09375
- key_weight: bfloat16 [4096, 1024], P(None, 'tp'), may hold values from -0.09375 to 0.09375
- value_weight: bfloat16 [4096, 1024], P(None, 'tp'), may hold values from -0.09375 to 0.09375
- out_weight: bfloat16 [4096, 4096], P('tp'), may hold values from -0.09375 to 0.09375
- links: int32 [32, 16], P('ctx'), may hold values from 0 to 31, as said below
- counts: int32 [32], P('ctx'), may hold values from 1 to 16, as said below
- doc_ids: int32 [32], replicated, may hold values from 0 to 7, never falling along the last dimension, each value on 1 to 8 neighbouring positions
Outputs:
- mixed: bfloat16 [4096, 4096], P(('ctx', 'tp'))
The draws below stay inside these ranges and needn't reach their ends.
Inputs may be any that keep to these rules, and one draw needn't show every extreme that they name: `links`: the first entry of each row is the query block itself; the entries of a row are distinct; every listed block lies within 4 ctx indices of its query block (block index // 4), and some query block of every ctx index lists a block exactly 4 indices away. `counts`: the first query block of each ctx index has 2 or more live slots, and block 0 has 16.
All inputs are finite; a program needn't handle non-finite values.
Results may differ from the reference program's by a relative error of at most 0.017.
Values may be sent and summed in bfloat16 or wider, within the bound.
A program may use at most 128 MiB of HBM per device.

```python
import math
import jax
import jax.numpy as jnp
import numpy as np
from jax import lax

D = 4096
HEADS = 32
KV_HEADS = 8
HEAD_DIM = 128
BLOCK = 128
LINKS = 16
REACH = 4
SEQ = 4096
NBLK = 32
BLK_DEV = 4
DOCS = 8
N_TP = 4


def draw_tokens(key, part):
    first = jax.random.fold_in(key, 0)
    base = jax.random.normal(first, (SEQ, D), jnp.float32)
    return jnp.clip(base, -6.0, 6.0).astype(jnp.bfloat16)


def draw_links(key, part):
    devices = NBLK // BLK_DEV
    width = (2 * REACH + 1) * BLK_DEV
    block = jnp.arange(NBLK, dtype=jnp.int32)[:, None]
    device = block // BLK_DEV
    offset = jnp.arange(width, dtype=jnp.int32)[None, :]
    candidate = (device - REACH) * BLK_DEV + offset
    first, second = jax.random.split(jax.random.fold_in(key, 11))
    noise = jax.random.randint(first, (NBLK, width), 0, 1 << 20)
    score = noise * 1024 + offset
    valid = (candidate >= 0) & (candidate < NBLK) & (candidate != block)
    target_device = jnp.where(device + REACH < devices, device + REACH, device - REACH)
    target = target_device * BLK_DEV + jax.random.randint(second, (NBLK, 1), 0, BLK_DEV)
    forced = (block % BLK_DEV == 0) & (candidate == target)
    score = jnp.where(valid, score, -1)
    score = jnp.where(forced, (1 << 30) + 5, score)
    chosen_score, chosen_index = lax.top_k(score, LINKS - 1)
    picked = jnp.take_along_axis(candidate, chosen_index, axis=1)
    return jnp.concatenate([block, picked], axis=1).astype(jnp.int32)


def draw_counts(key, part):
    drawn = jax.random.randint(jax.random.fold_in(key, 23), (NBLK,), 1, LINKS + 1)
    leading = jnp.arange(NBLK, dtype=jnp.int32) % BLK_DEV == 0
    drawn = jnp.where(leading, jnp.maximum(drawn, 2), drawn)
    return drawn.at[0].set(LINKS).astype(jnp.int32)


def steps_of(rng, dims, pieces, least, largest):
    def one(dim, parts):
        steps = jax.random.uniform(jax.random.fold_in(jax.random.fold_in(rng, 6), dim), (parts,), jnp.float32, least / len(pieces), largest / len(pieces))
        return jnp.repeat(jnp.exp(steps), dims[dim] // parts).reshape((-1,) + (1,) * (len(dims) - dim - 1))

    level = one(*pieces[0])
    for cut in pieces[1:]:
        level = level * one(*cut)
    return level


def length_profile(count, total, reach, lean):
    weights = [(1 << 20) // math.isqrt(standing ** lean) + 1 for standing in range(2, count + 1)]
    rest, holding = total - reach - (count - 1), [1] * (count - 1)
    while rest > 0:
        movable = [i for i in range(count - 1) if holding[i] < reach]
        whole, remaining = sum([weights[i] for i in movable]), rest
        for i in movable:
            extra = min(reach - holding[i], max(1, remaining * weights[i] // whole), rest)
            holding[i] = holding[i] + extra
            rest = rest - extra
    return np.array([reach] + holding)


def ragged_sizes(key, count, total, reach, lean):
    if count == 2:
        one = jax.random.randint(key, (), max(1, total - reach), min(reach, total - 1) + 1)
        return jnp.stack([one, total - one])
    tallies = jnp.asarray(length_profile(count, total, reach, lean), jnp.int32)
    twos = (count - 1) // 2
    donor, receiver = tallies[1:1 + 2 * twos:2], tallies[2:2 + 2 * twos:2]
    slack = jnp.minimum(donor - 1, reach - receiver)
    passed = jax.random.randint(jax.random.fold_in(key, 1), (twos,), 0, 1 << 20) % (slack + 1)
    tallies = tallies.at[1:1 + 2 * twos:2].set(donor - passed).at[2:2 + 2 * twos:2].set(receiver + passed)
    return tallies[jax.random.permutation(jax.random.fold_in(key, 2), count)]


def bell_draw(rng, extent, scale, bound, cuts=(), kind=jnp.bfloat16):
    values = scale * jax.random.normal(rng, extent, jnp.float32)
    if cuts:
        values = values * steps_of(rng, extent, cuts, -0.22, 0.18)
    return jnp.clip(values, -bound, bound).astype(kind)


def setup_inputs(seed: int = 0) -> dict:
    streams_of = jax.random.split(jax.random.key(seed), 9)
    return {
        "tokens": draw_tokens(jax.random.fold_in(streams_of[8], 71), 0),
        "query_weight": bell_draw(streams_of[1], (D, HEADS * HEAD_DIM), D ** -0.5, 0.09375, ((1, 4),)),
        "key_weight": bell_draw(streams_of[2], (D, KV_HEADS * HEAD_DIM), D ** -0.5, 0.09375, ((1, 4),)),
        "value_weight": bell_draw(streams_of[3], (D, KV_HEADS * HEAD_DIM), D ** -0.5, 0.09375, ((1, 4),)),
        "out_weight": bell_draw(streams_of[4], (HEADS * HEAD_DIM, D), (HEADS * HEAD_DIM) ** -0.5, 0.09375, ((0, 4),)),
        "links": draw_links(jax.random.fold_in(streams_of[8], 71), 0),
        "counts": draw_counts(jax.random.fold_in(streams_of[8], 71), 0),
        "doc_ids": jnp.searchsorted(jnp.cumsum(ragged_sizes(streams_of[7], DOCS, NBLK, 8, 0)), jnp.arange(NBLK), side="right").astype(jnp.int32),
    }


def reference(tokens, query_weight, key_weight, value_weight, out_weight, links, counts, doc_ids):
    query = jnp.dot(tokens, query_weight, preferred_element_type=jnp.float32).astype(jnp.bfloat16)
    keys = jnp.dot(tokens, key_weight, preferred_element_type=jnp.float32).astype(jnp.bfloat16)
    values = jnp.dot(tokens, value_weight, preferred_element_type=jnp.float32).astype(jnp.bfloat16)
    group = HEADS // KV_HEADS
    query_blocks = query.reshape(NBLK, BLOCK, KV_HEADS, group, HEAD_DIM)
    key_blocks = keys.reshape(NBLK, BLOCK, KV_HEADS, HEAD_DIM)
    value_blocks = values.reshape(NBLK, BLOCK, KV_HEADS, HEAD_DIM)
    causal = jnp.arange(BLOCK)[None, :] <= jnp.arange(BLOCK)[:, None]

    def one_block(index):
        listed = links[index]
        chosen_keys = jnp.take(key_blocks, listed, axis=0, mode="clip").astype(jnp.float32)
        chosen_values = jnp.take(value_blocks, listed, axis=0, mode="clip").astype(jnp.float32)
        live = jnp.arange(LINKS) < counts[index]
        other_doc = jnp.take(doc_ids, listed, mode="clip") != doc_ids[index]
        earlier = (listed < index) | other_doc
        same = listed == index
        allowed = live[None, :, None] & (earlier[None, :, None] | (same[None, :, None] & causal[:, None, :]))
        scores = jnp.einsum("qhgd,skhd->hgqsk", query_blocks[index].astype(jnp.float32), chosen_keys) * (HEAD_DIM ** -0.5)
        scores = jnp.where(allowed, scores, -1e30)
        top = jnp.max(scores, axis=(3, 4), keepdims=True)
        powers = jnp.where(allowed, jnp.exp(scores - top), 0.0)
        total = jnp.sum(powers, axis=(3, 4), keepdims=True)
        weights = (powers / total).astype(jnp.bfloat16).astype(jnp.float32)
        result = jnp.einsum("hgqsk,skhd->qhgd", weights, chosen_values)
        return result.astype(jnp.bfloat16)

    attended = lax.map(one_block, jnp.arange(NBLK, dtype=jnp.int32)).reshape(SEQ, HEADS * HEAD_DIM)
    width = HEADS * HEAD_DIM // N_TP
    mixed = jnp.zeros((SEQ, D), jnp.float32)
    for part_index in range(N_TP):
        term = jnp.dot(attended[:, part_index * width:(part_index + 1) * width], out_weight[part_index * width:(part_index + 1) * width], preferred_element_type=jnp.float32)
        mixed = mixed + term.astype(jnp.bfloat16).astype(jnp.float32)
    return mixed.astype(jnp.bfloat16)
```

```python
import functools

import jax
import jax.numpy as jnp
from jax import lax
from jax.experimental import pallas as pl
from jax.experimental.pallas import tpu as pltpu
from jax.sharding import PartitionSpec as P

HEAD_DIM = 128
BLOCK = 128
LINKS = 16
REACH = 4
CORES = 2
BF16 = jnp.bfloat16
F32 = jnp.float32
VMEM = pl.BlockSpec(memory_space=pltpu.VMEM)
SMEM = pl.BlockSpec(memory_space=pltpu.SMEM)
ANY = pl.BlockSpec(memory_space=pl.ANY)
GRANT = 56 * 1024 * 1024


def attend_kernel(
    blocks, kv_heads, group, place_ref, links_ref, counts_ref, docs_ref, query_ref, source_ref,
    out_ref, key_buf, value_buf, score_buf, sum_buf, acc_buf, live_ref, sems
):
    first, anchor = place_ref[0], place_ref[1]

    def copies(block, position, listed):
        at = listed - anchor
        rows = pl.ds(pl.multiple_of(position * BLOCK, BLOCK), BLOCK)
        return (
            pltpu.make_async_copy(
                source_ref.at[at, 0], key_buf.at[block, rows], sems.at[block, position, 0]
            ),
            pltpu.make_async_copy(
                source_ref.at[at, 1], value_buf.at[block, rows], sems.at[block, position, 1]
            ),
        )

    for block in range(blocks):
        mine = first + block
        doc = docs_ref[mine]

        def pick(slot, position, block=block, mine=mine, doc=doc):
            listed = links_ref[block, slot]
            seen = (slot < counts_ref[block]) & (
                (listed <= mine) | (docs_ref[listed] != doc)
            )

            @pl.when(seen)
            def _():
                for copy in copies(block, position, listed):
                    copy.start()

            return position + seen.astype(jnp.int32)

        live = lax.fori_loop(0, LINKS, pick, jnp.int32(0))
        live_ref[block] = live

        @pl.when(lax.rem(live, 2) == 1)
        def _(block=block, mine=mine, live=live):
            for copy in copies(block, live, mine):
                copy.start()

    scale = HEAD_DIM ** (-0.5) * 1.4426950408889634
    pair = 2 * BLOCK
    height = group * BLOCK
    token = lax.rem(lax.broadcasted_iota(jnp.int32, (height, pair), 0), BLOCK)
    column = lax.broadcasted_iota(jnp.int32, (height, pair), 1)
    row_column = lax.broadcasted_iota(jnp.int32, (1, pair), 1)

    def one(block, carry):
        live = live_ref[block]
        pairs = lax.div(live + 1, 2)

        def land(position, carry):
            for copy in copies(block, position, anchor):
                copy.wait()
            return carry

        lax.fori_loop(0, pairs * 2, land, 0)
        rows = pl.ds(pl.multiple_of(block * BLOCK, BLOCK), BLOCK)
        for head in range(kv_heads):
            lanes = pl.ds(head * HEAD_DIM, HEAD_DIM)
            query = jnp.concatenate(
                [
                    query_ref[rows, pl.ds((head * group + member) * HEAD_DIM, HEAD_DIM)]
                    for member in range(group)
                ],
                axis=0,
            )

            def scores_of(index):
                keys = key_buf[block, pl.ds(pl.multiple_of(index * pair, pair), pair), lanes]
                scores = lax.dot_general(
                    query, keys, (((1,), (1,)), ((), ())), preferred_element_type=F32
                )
                bound = (live - index * 2) * BLOCK
                return scores * scale + jnp.where(row_column < bound, 0.0, -1e30)

            def halves_max(scores):
                return jnp.maximum(scores[:, :BLOCK], scores[:, BLOCK:])

            scores = scores_of(0)
            scores = jnp.where((column >= BLOCK) | (column <= token), scores, -1e30)
            score_buf[0] = scores

            def first_pass(index, top):
                scores = scores_of(index)
                score_buf[index] = scores
                return jnp.maximum(top, halves_max(scores))

            top = lax.fori_loop(1, pairs, first_pass, halves_max(scores))
            top = jnp.max(top, axis=1, keepdims=True)
            acc_buf[...] = jnp.zeros_like(acc_buf)
            sum_buf[...] = jnp.zeros_like(sum_buf)

            def second_pass(index, carry):
                powers = jnp.exp2(score_buf[index] - top)
                sum_buf[...] += powers[:, :BLOCK] + powers[:, BLOCK:]
                values = value_buf[block, pl.ds(pl.multiple_of(index * pair, pair), pair), lanes]
                acc_buf[...] += jnp.dot(
                    powers.astype(BF16), values, preferred_element_type=F32
                )
                return carry

            lax.fori_loop(0, pairs, second_pass, 0)
            total = jnp.sum(sum_buf[...], axis=1, keepdims=True)
            result = (acc_buf[...] / total).astype(BF16)
            for member in range(group):
                out_ref[rows, pl.ds((head * group + member) * HEAD_DIM, HEAD_DIM)] = result[
                    member * BLOCK : (member + 1) * BLOCK
                ]
        return carry

    lax.fori_loop(0, blocks, one, 0)


def attend(place, links, counts, doc_ids, query, source):
    row_count, query_width = query.shape
    key_width = source.shape[3]
    blocks = row_count // BLOCK
    kv_heads = key_width // HEAD_DIM
    group = query_width // key_width
    keys = LINKS * BLOCK
    height = group * BLOCK
    return pl.pallas_call(
        functools.partial(attend_kernel, blocks, kv_heads, group),
        out_shape=jax.ShapeDtypeStruct(query.shape, BF16),
        in_specs=[SMEM] * 4 + [VMEM, ANY],
        out_specs=VMEM,
        scratch_shapes=[
            pltpu.VMEM((blocks, keys, key_width), BF16),
            pltpu.VMEM((blocks, keys, key_width), BF16),
            pltpu.VMEM((LINKS // 2, height, 2 * BLOCK), F32),
            pltpu.VMEM((height, BLOCK), F32),
            pltpu.VMEM((height, HEAD_DIM), F32),
            pltpu.SMEM((blocks,), jnp.int32),
            pltpu.SemaphoreType.DMA((blocks, LINKS, 2)),
        ],
        compiler_params=pltpu.CompilerParams(vmem_limit_bytes=GRANT),
        cost_estimate=pl.CostEstimate(
            flops=4 * row_count * query_width * keys, bytes_accessed=1 << 23, transcendentals=0
        ),
    )(place, links, counts, doc_ids, query, source)


def project_kernel(
    tp, chunks, wide, attended_ref, weight_ref, out_ref, weight_buf, part_buf, own_buf,
    mate_send, mate_recv, far_send, far_recv, weight_sems, mate_send_sems, mate_recv_sems,
    far_send_sems, far_recv_sems
):
    rows = attended_ref.shape[0] // tp
    across = tp // CORES
    me = lax.axis_index("tp")
    chip, core = lax.div(me, CORES), lax.rem(me, CORES)
    mate = chip * CORES + 1 - core

    def weight_copy(index):
        columns = pl.ds(pl.multiple_of(index * wide, wide), wide)
        return pltpu.make_async_copy(
            weight_ref.at[:, columns], weight_buf.at[index], weight_sems.at[index]
        )

    def start_weight(index, carry):
        weight_copy(index).start()
        return carry

    lax.fori_loop(0, chunks, start_weight, 0)

    barrier = pltpu.get_barrier_semaphore()
    pl.semaphore_signal(barrier, inc=1, device_id={"tp": mate})
    for step in range(1, across):
        other = lax.rem(chip + step, across) * CORES + core
        pl.semaphore_signal(barrier, inc=1, device_id={"tp": other})
    pl.semaphore_wait(barrier, across)

    def mate_copy(index):
        return pltpu.make_async_remote_copy(
            src_ref=mate_send.at[index],
            dst_ref=mate_recv.at[index],
            send_sem=mate_send_sems.at[index],
            recv_sem=mate_recv_sems.at[index],
            device_id={"tp": mate},
        )

    def far_copy(index, step):
        other = lax.rem(chip + step, across) * CORES + core
        return pltpu.make_async_remote_copy(
            src_ref=far_send.at[index, step - 1],
            dst_ref=far_recv.at[index, step - 1],
            send_sem=far_send_sems.at[index, step - 1],
            recv_sem=far_recv_sems.at[index, step - 1],
            device_id={"tp": other},
        )

    def rows_of(step, which):
        start = (lax.rem(chip + step, across) * CORES + which) * rows
        return pl.ds(pl.multiple_of(start, rows), rows)

    def multiply(index):
        weight_copy(index).wait()
        part_buf[lax.rem(index, 2)] = jnp.dot(
            attended_ref[...], weight_buf[index], preferred_element_type=F32
        )
        for step in range(across):
            mate_send[index, step] = part_buf[
                lax.rem(index, 2), rows_of(step, 1 - core)
            ].astype(BF16)
        mate_copy(index).start()

    def combine(index):
        mate_copy(index).wait_recv()
        for step in range(across):
            total = part_buf[lax.rem(index, 2), rows_of(step, core)] + mate_recv[
                index, step
            ].astype(F32)
            if step == 0:
                own_buf[index] = total
            else:
                far_send[index, step - 1] = total.astype(BF16)
                far_copy(index, step).start()

    multiply(0)

    def middle(index, carry):
        multiply(index)
        combine(index - 1)
        return carry

    lax.fori_loop(1, chunks, middle, 0)
    combine(chunks - 1)

    def finish(index, carry):
        total = own_buf[index]
        for step in range(1, across):
            far_copy(index, step).wait_recv()
            total = total + far_recv[index, step - 1].astype(F32)
        columns = pl.ds(pl.multiple_of(index * wide, wide), wide)
        out_ref[:, columns] = total.astype(BF16)
        return carry

    lax.fori_loop(0, chunks, finish, 0)

    def drain(index, carry):
        mate_copy(index).wait_send()
        for step in range(1, across):
            far_copy(index, step).wait_send()
        return carry

    lax.fori_loop(0, chunks, drain, 0)


def project(attended, out_weight):
    tp = lax.axis_size("tp")
    across = tp // CORES
    row_count, depth = attended.shape
    width = out_weight.shape[1]
    rows = row_count // tp
    wide = min(512, width)
    chunks = width // wide
    return pl.pallas_call(
        functools.partial(project_kernel, tp, chunks, wide),
        out_shape=jax.ShapeDtypeStruct((rows, width), BF16),
        in_specs=[VMEM, ANY],
        out_specs=VMEM,
        scratch_shapes=[
            pltpu.VMEM((chunks, depth, wide), BF16),
            pltpu.VMEM((2, row_count, wide), F32),
            pltpu.VMEM((chunks, rows, wide), F32),
            pltpu.VMEM((chunks, across, rows, wide), BF16),
            pltpu.VMEM((chunks, across, rows, wide), BF16),
            pltpu.VMEM((chunks, across - 1, rows, wide), BF16),
            pltpu.VMEM((chunks, across - 1, rows, wide), BF16),
            pltpu.SemaphoreType.DMA((chunks,)),
            pltpu.SemaphoreType.DMA((chunks,)),
            pltpu.SemaphoreType.DMA((chunks,)),
            pltpu.SemaphoreType.DMA((chunks, across - 1)),
            pltpu.SemaphoreType.DMA((chunks, across - 1)),
        ],
        compiler_params=pltpu.CompilerParams(
            collective_id=1, has_side_effects=True, vmem_limit_bytes=GRANT
        ),
        cost_estimate=pl.CostEstimate(
            flops=2 * row_count * depth * width, bytes_accessed=1 << 24, transcendentals=0
        ),
    )(attended, out_weight)


def from_behind(block, axis, distance):
    devices = range(lax.axis_size(axis))
    route = [(i - distance, i) for i in devices if i - distance in devices]
    return lax.ppermute(block, axis, route)


def local(tokens, query_weight, key_weight, value_weight, out_weight, links, counts, doc_ids):
    row_count = tokens.shape[0]
    key_width = key_weight.shape[1]
    piece = lax.all_gather(tokens, "tp", axis=1, tiled=True)
    weights = (query_weight, key_weight, value_weight)
    query, keys, values = tuple(
        jnp.dot(piece, weight, preferred_element_type=F32).astype(BF16) for weight in weights
    )
    block_count = row_count // BLOCK
    stacked = jnp.stack(
        [keys.reshape(block_count, BLOCK, key_width), values.reshape(block_count, BLOCK, key_width)],
        axis=1,
    )
    position = lax.axis_index("ctx")
    pieces = []
    for offset in range(-REACH, REACH + 1):
        if offset == 0:
            pieces.append(stacked)
        else:
            pieces.append(from_behind(stacked, "ctx", -offset))
    source = jnp.concatenate(pieces, axis=0)
    place = jnp.stack([position * block_count, (position - REACH) * block_count]).astype(jnp.int32)
    attended = attend(place, links, counts, doc_ids, query, source)
    return project(attended, out_weight)


def solution(mesh):
    placed = (
        P("ctx", "tp"),
        P(None, "tp"),
        P(None, "tp"),
        P(None, "tp"),
        P("tp", None),
        P("ctx", None),
        P("ctx"),
        P(),
    )
    return jax.shard_map(
        local, mesh=mesh, in_specs=placed, out_specs=P(("ctx", "tp"), None), check_vma=False
    )
```

```python
import functools

import jax
import jax.numpy as jnp
from jax import lax
from jax.experimental import pallas as pl
from jax.experimental.pallas import tpu as pltpu
from jax.sharding import PartitionSpec as P

HEAD_DIM = 128
BLOCK = 128
LINKS = 16
REACH = 4
CORES = 2
BF16 = jnp.bfloat16
F32 = jnp.float32
VMEM = pl.BlockSpec(memory_space=pltpu.VMEM)
SMEM = pl.BlockSpec(memory_space=pltpu.SMEM)
ANY = pl.BlockSpec(memory_space=pl.ANY)
GRANT = 56 * 1024 * 1024


def attend_kernel(
    blocks, kv_heads, group, place_ref, links_ref, counts_ref, docs_ref, query_ref, source_ref,
    out_ref, key_buf, value_buf, score_buf, sum_buf, acc_buf, live_ref, sems
):
    first, anchor = place_ref[0], place_ref[1]

    def copies(block, position, listed):
        at = listed - anchor
        rows = pl.ds(pl.multiple_of(position * BLOCK, BLOCK), BLOCK)
        return (
            pltpu.make_async_copy(
                source_ref.at[at, 0], key_buf.at[block, rows], sems.at[block, position, 0]
            ),
            pltpu.make_async_copy(
                source_ref.at[at, 1], value_buf.at[block, rows], sems.at[block, position, 1]
            ),
        )

    for block in range(blocks):
        mine = first + block
        doc = docs_ref[mine]

        def pick(slot, position, block=block, mine=mine, doc=doc):
            listed = links_ref[block, slot]
            seen = (slot < counts_ref[block]) & (
                (listed <= mine) | (docs_ref[listed] != doc)
            )

            @pl.when(seen)
            def _():
                for copy in copies(block, position, listed):
                    copy.start()

            return position + seen.astype(jnp.int32)

        live = lax.fori_loop(0, LINKS, pick, jnp.int32(0))
        live_ref[block] = live

        @pl.when(lax.rem(live, 2) == 1)
        def _(block=block, mine=mine, live=live):
            for copy in copies(block, live, mine):
                copy.start()

    scale = HEAD_DIM ** (-0.5) * 1.4426950408889634
    pair = 2 * BLOCK
    height = group * BLOCK
    token = lax.rem(lax.broadcasted_iota(jnp.int32, (height, pair), 0), BLOCK)
    column = lax.broadcasted_iota(jnp.int32, (height, pair), 1)
    row_column = lax.broadcasted_iota(jnp.int32, (1, pair), 1)

    def one(block, carry):
        live = live_ref[block]
        pairs = lax.div(live + 1, 2)

        def land(position, carry):
            for copy in copies(block, position, anchor):
                copy.wait()
            return carry

        lax.fori_loop(0, pairs * 2, land, 0)
        rows = pl.ds(pl.multiple_of(block * BLOCK, BLOCK), BLOCK)
        for head in range(kv_heads):
            lanes = pl.ds(head * HEAD_DIM, HEAD_DIM)
            query = jnp.concatenate(
                [
                    query_ref[rows, pl.ds((head * group + member) * HEAD_DIM, HEAD_DIM)]
                    for member in range(group)
                ],
                axis=0,
            )

            def scores_of(index):
                keys = key_buf[block, pl.ds(pl.multiple_of(index * pair, pair), pair), lanes]
                scores = lax.dot_general(
                    query, keys, (((1,), (1,)), ((), ())), preferred_element_type=F32
                )
                bound = (live - index * 2) * BLOCK
                return scores * scale + jnp.where(row_column < bound, 0.0, -1e30)

            def halves_max(scores):
                return jnp.maximum(scores[:, :BLOCK], scores[:, BLOCK:])

            scores = scores_of(0)
            scores = jnp.where((column >= BLOCK) | (column <= token), scores, -1e30)
            score_buf[0] = scores

            def first_pass(index, top):
                scores = scores_of(index)
                score_buf[index] = scores
                return jnp.maximum(top, halves_max(scores))

            top = lax.fori_loop(1, pairs, first_pass, halves_max(scores))
            top = jnp.max(top, axis=1, keepdims=True)
            acc_buf[...] = jnp.zeros_like(acc_buf)
            sum_buf[...] = jnp.zeros_like(sum_buf)

            def second_pass(index, carry):
                powers = jnp.exp2(score_buf[index] - top)
                sum_buf[...] += powers[:, :BLOCK] + powers[:, BLOCK:]
                values = value_buf[block, pl.ds(pl.multiple_of(index * pair, pair), pair), lanes]
                acc_buf[...] += jnp.dot(
                    powers.astype(BF16), values, preferred_element_type=F32
                )
                return carry

            lax.fori_loop(0, pairs, second_pass, 0)
            total = jnp.sum(sum_buf[...], axis=1, keepdims=True)
            result = (acc_buf[...] / total).astype(BF16)
            for member in range(group):
                out_ref[rows, pl.ds((head * group + member) * HEAD_DIM, HEAD_DIM)] = result[
                    member * BLOCK : (member + 1) * BLOCK
                ]
        return carry

    lax.fori_loop(0, blocks, one, 0)


def attend(place, links, counts, doc_ids, query, source):
    row_count, query_width = query.shape
    key_width = source.shape[3]
    blocks = row_count // BLOCK
    kv_heads = key_width // HEAD_DIM
    group = query_width // key_width
    keys = LINKS * BLOCK
    height = group * BLOCK
    return pl.pallas_call(
        functools.partial(attend_kernel, blocks, kv_heads, group),
        out_shape=jax.ShapeDtypeStruct(query.shape, BF16),
        in_specs=[SMEM] * 4 + [VMEM, ANY],
        out_specs=VMEM,
        scratch_shapes=[
            pltpu.VMEM((blocks, keys, key_width), BF16),
            pltpu.VMEM((blocks, keys, key_width), BF16),
            pltpu.VMEM((LINKS // 2, height, 2 * BLOCK), F32),
            pltpu.VMEM((height, BLOCK), F32),
            pltpu.VMEM((height, HEAD_DIM), F32),
            pltpu.SMEM((blocks,), jnp.int32),
            pltpu.SemaphoreType.DMA((blocks, LINKS, 2)),
        ],
        compiler_params=pltpu.CompilerParams(vmem_limit_bytes=GRANT),
        cost_estimate=pl.CostEstimate(
            flops=4 * row_count * query_width * keys, bytes_accessed=1 << 23, transcendentals=0
        ),
    )(place, links, counts, doc_ids, query, source)


def project_kernel(
    tp, chunks, wide, attended_ref, weight_ref, out_ref, weight_buf, part_buf, own_buf,
    mate_send, mate_recv, far_send, far_recv, weight_sems, mate_send_sems, mate_recv_sems,
    far_send_sems, far_recv_sems
):
    rows = attended_ref.shape[0] // tp
    across = tp // CORES
    me = lax.axis_index("tp")
    chip, core = lax.div(me, CORES), lax.rem(me, CORES)
    mate = chip * CORES + 1 - core

    def weight_copy(index):
        columns = pl.ds(pl.multiple_of(index * wide, wide), wide)
        return pltpu.make_async_copy(
            weight_ref.at[:, columns], weight_buf.at[index], weight_sems.at[index]
        )

    def start_weight(index, carry):
        weight_copy(index).start()
        return carry

    lax.fori_loop(0, chunks, start_weight, 0)

    barrier = pltpu.get_barrier_semaphore()
    pl.semaphore_signal(barrier, inc=1, device_id={"tp": mate})
    for step in range(1, across):
        other = lax.rem(chip + step, across) * CORES + core
        pl.semaphore_signal(barrier, inc=1, device_id={"tp": other})
    pl.semaphore_wait(barrier, across)

    def mate_copy(index):
        return pltpu.make_async_remote_copy(
            src_ref=mate_send.at[index],
            dst_ref=mate_recv.at[index],
            send_sem=mate_send_sems.at[index],
            recv_sem=mate_recv_sems.at[index],
            device_id={"tp": mate},
        )

    def far_copy(index, step):
        other = lax.rem(chip + step, across) * CORES + core
        return pltpu.make_async_remote_copy(
            src_ref=far_send.at[index, step - 1],
            dst_ref=far_recv.at[index, step - 1],
            send_sem=far_send_sems.at[index, step - 1],
            recv_sem=far_recv_sems.at[index, step - 1],
            device_id={"tp": other},
        )

    def rows_of(step, which):
        start = (lax.rem(chip + step, across) * CORES + which) * rows
        return pl.ds(pl.multiple_of(start, rows), rows)

    def multiply(index):
        weight_copy(index).wait()
        part_buf[lax.rem(index, 2)] = jnp.dot(
            attended_ref[...], weight_buf[index], preferred_element_type=F32
        )
        for step in range(across):
            mate_send[index, step] = part_buf[
                lax.rem(index, 2), rows_of(step, 1 - core)
            ].astype(BF16)
        mate_copy(index).start()

    def combine(index):
        mate_copy(index).wait_recv()
        for step in range(across):
            total = part_buf[lax.rem(index, 2), rows_of(step, core)] + mate_recv[
                index, step
            ].astype(F32)
            if step == 0:
                own_buf[index] = total
            else:
                far_send[index, step - 1] = total.astype(BF16)
                far_copy(index, step).start()

    multiply(0)

    def middle(index, carry):
        multiply(index)
        combine(index - 1)
        return carry

    lax.fori_loop(1, chunks, middle, 0)
    combine(chunks - 1)

    def finish(index, carry):
        total = own_buf[index]
        for step in range(1, across):
            far_copy(index, step).wait_recv()
            total = total + far_recv[index, step - 1].astype(F32)
        columns = pl.ds(pl.multiple_of(index * wide, wide), wide)
        out_ref[:, columns] = total.astype(BF16)
        return carry

    lax.fori_loop(0, chunks, finish, 0)

    def drain(index, carry):
        mate_copy(index).wait_send()
        for step in range(1, across):
            far_copy(index, step).wait_send()
        return carry

    lax.fori_loop(0, chunks, drain, 0)


def project(attended, out_weight):
    tp = lax.axis_size("tp")
    across = tp // CORES
    row_count, depth = attended.shape
    width = out_weight.shape[1]
    rows = row_count // tp
    wide = min(512, width)
    chunks = width // wide
    return pl.pallas_call(
        functools.partial(project_kernel, tp, chunks, wide),
        out_shape=jax.ShapeDtypeStruct((rows, width), BF16),
        in_specs=[VMEM, ANY],
        out_specs=VMEM,
        scratch_shapes=[
            pltpu.VMEM((chunks, depth, wide), BF16),
            pltpu.VMEM((2, row_count, wide), F32),
            pltpu.VMEM((chunks, rows, wide), F32),
            pltpu.VMEM((chunks, across, rows, wide), BF16),
            pltpu.VMEM((chunks, across, rows, wide), BF16),
            pltpu.VMEM((chunks, across - 1, rows, wide), BF16),
            pltpu.VMEM((chunks, across - 1, rows, wide), BF16),
            pltpu.SemaphoreType.DMA((chunks,)),
            pltpu.SemaphoreType.DMA((chunks,)),
            pltpu.SemaphoreType.DMA((chunks,)),
            pltpu.SemaphoreType.DMA((chunks, across - 1)),
            pltpu.SemaphoreType.DMA((chunks, across - 1)),
        ],
        compiler_params=pltpu.CompilerParams(
            collective_id=1, has_side_effects=True, vmem_limit_bytes=GRANT
        ),
        cost_estimate=pl.CostEstimate(
            flops=2 * row_count * depth * width, bytes_accessed=1 << 24, transcendentals=0
        ),
    )(attended, out_weight)


def gather_kernel(
    tp, ctx, hops, tokens_ref, query_weight_ref, key_weight_ref, value_weight_ref,
    query_ref, source_ref, token_buf, query_weight, key_weight, value_weight, stage,
    load_sems, weight_sems, store_sems, y_send, y_recv, m_send, m_recv,
    x_send, x_recv, full_send, full_recv, half_send, half_recv, k_send, k_recv
):
    blocks = tokens_ref.shape[0] // BLOCK
    across = tp // CORES
    depth = tokens_ref.shape[1]
    pairs = ctx // 2
    me = lax.axis_index("tp")
    chip, core = lax.div(me, CORES), lax.rem(me, CORES)
    mate = chip * CORES + 1 - core
    here = lax.axis_index("ctx")
    pair, side = lax.div(here, 2), lax.rem(here, 2)
    beside = pair * 2 + 1 - side
    ways = (1, -1)

    def exists(offset):
        return (pair + offset >= 0) & (pair + offset < pairs)

    def needed(offset, holder, reader):
        distance = 2 * offset + holder - reader
        return (distance <= REACH) & (distance >= -REACH)

    def slot(offset, holder):
        return (offset + hops) * 2 + holder

    def peer(step):
        return lax.rem(chip + step, across) * CORES + core

    def rows_of(block):
        return pl.ds(pl.multiple_of(block * BLOCK, BLOCK), BLOCK)

    def load(block):
        return pltpu.make_async_copy(
            tokens_ref.at[rows_of(block)], token_buf.at[me, block], load_sems.at[block]
        )

    def y_copy(block, step):
        return pltpu.make_async_remote_copy(
            src_ref=tokens_ref.at[rows_of(block)],
            dst_ref=token_buf.at[me, block],
            send_sem=y_send.at[step - 1, block],
            recv_sem=y_recv.at[step - 1, block],
            device_id={"tp": peer(step)},
        )

    def m_copy(block, step):
        owner = peer(across - step)
        if step == 0:
            source, owner = tokens_ref.at[rows_of(block)], me
        else:
            source = token_buf.at[owner, block]
        return pltpu.make_async_remote_copy(
            src_ref=source,
            dst_ref=token_buf.at[owner, block],
            send_sem=m_send.at[step, block],
            recv_sem=m_recv.at[step, block],
            device_id={"tp": mate},
        )

    weight_copies = [
        pltpu.make_async_copy(key_weight_ref, key_weight, weight_sems.at[0]),
        pltpu.make_async_copy(value_weight_ref, value_weight, weight_sems.at[1]),
        pltpu.make_async_copy(query_weight_ref, query_weight, weight_sems.at[2]),
    ]

    def begin(block, carry):
        load(block).start()
        return carry

    lax.fori_loop(0, blocks, begin, 0)
    for copy in weight_copies:
        copy.start()

    barrier = pltpu.get_barrier_semaphore()
    pl.semaphore_signal(barrier, inc=1, device_id={"tp": mate})
    for step in range(1, across):
        pl.semaphore_signal(barrier, inc=1, device_id={"tp": peer(step)})
    pl.semaphore_signal(barrier, inc=1, device_id={"ctx": beside})
    for way in ways:

        @pl.when(exists(way))
        def _(way=way):
            pl.semaphore_signal(barrier, inc=1, device_id={"ctx": here + 2 * way})

    expected = across + 1 + exists(1).astype(jnp.int32) + exists(-1).astype(jnp.int32)
    pl.semaphore_wait(barrier, expected)

    def push(block, carry):
        for step in range(1, across):
            y_copy(block, step).start()
        m_copy(block, 0).start()
        return carry

    lax.fori_loop(0, blocks, push, 0)

    def store(block):
        return pltpu.make_async_copy(
            stage.at[block], source_ref.at[slot(0, side), block], store_sems.at[block]
        )

    def x_copy(block):
        return pltpu.make_async_remote_copy(
            src_ref=stage.at[block],
            dst_ref=source_ref.at[slot(0, side), block],
            send_sem=x_send.at[block],
            recv_sem=x_recv.at[block],
            device_id={"ctx": beside},
        )

    def full_copy(block, way, hop):
        source = stage.at[block] if hop == 1 else source_ref.at[slot(-way * (hop - 1), side), block]
        return pltpu.make_async_remote_copy(
            src_ref=source,
            dst_ref=source_ref.at[slot(-way * hop, side), block],
            send_sem=full_send.at[ways.index(way), hop - 1, block],
            recv_sem=full_recv.at[ways.index(way), hop - 1, block],
            device_id={"ctx": here + 2 * way},
        )

    def half_copy(block, way, hop):
        return pltpu.make_async_remote_copy(
            src_ref=source_ref.at[slot(-way * (hop - 1), 1 - side), block, 1],
            dst_ref=source_ref.at[slot(-way * hop, 1 - side), block, 1],
            send_sem=half_send.at[ways.index(way), hop - 1, block],
            recv_sem=half_recv.at[ways.index(way), hop - 1, block],
            device_id={"ctx": here + 2 * way},
        )

    def k_copy(block, way, hop):
        return pltpu.make_async_remote_copy(
            src_ref=source_ref.at[slot(-way * hop, side), block, 0],
            dst_ref=source_ref.at[slot(-way * hop, side), block, 0],
            send_sem=k_send.at[ways.index(way), hop - 1, block],
            recv_sem=k_recv.at[ways.index(way), hop - 1, block],
            device_id={"ctx": beside},
        )

    def full_sent(way, hop):
        return exists(way) & exists(-way * (hop - 1))

    def full_due(way, hop):
        return exists(-way * hop)

    def half_sent(way, hop):
        return full_sent(way, hop) & needed(-way * hop, 1 - side, side)

    def half_due(way, hop):
        return full_due(way, hop) & needed(-way * hop, 1 - side, side)

    def k_sent(way, hop):
        return full_due(way, hop) & needed(-way * hop, side, 1 - side)

    def k_due(way, hop):
        return full_due(way, hop) & needed(-way * hop, 1 - side, side)

    def k_received(block, way, hop):
        return pltpu.make_async_remote_copy(
            src_ref=source_ref.at[slot(-way * hop, 1 - side), block, 0],
            dst_ref=source_ref.at[slot(-way * hop, 1 - side), block, 0],
            send_sem=k_send.at[ways.index(way), hop - 1, block],
            recv_sem=k_recv.at[ways.index(way), hop - 1, block],
            device_id={"ctx": beside},
        )

    def multiply(block, weight, lanes):
        return sum(
            jnp.dot(
                token_buf[part, block],
                weight[part * depth : (part + 1) * depth, lanes],
                preferred_element_type=F32,
            )
            for part in range(tp)
        ).astype(BF16)

    def make(block):
        for step in range(1, across):
            y_copy_in(block, step).wait_recv()
            m_copy(block, step).start()
        load(block).wait()
        for step in range(across):
            m_copy_in(block, step).wait_recv()

        @pl.when(block == 0)
        def _():
            weight_copies[0].wait()
            weight_copies[1].wait()

        stage[block, 0] = multiply(block, key_weight, slice(None))
        stage[block, 1] = multiply(block, value_weight, slice(None))
        for way in ways:

            @pl.when(full_sent(way, 1))
            def _(way=way):
                full_copy(block, way, 1).start()

        x_copy(block).start()
        store(block).start()

    def y_copy_in(block, step):
        owner = peer(across - step)
        return pltpu.make_async_remote_copy(
            src_ref=tokens_ref.at[rows_of(block)],
            dst_ref=token_buf.at[owner, block],
            send_sem=y_send.at[step - 1, block],
            recv_sem=y_recv.at[step - 1, block],
            device_id={"tp": peer(step)},
        )

    def m_copy_in(block, step):
        owner = lax.rem(chip + across - step, across) * CORES + 1 - core
        return pltpu.make_async_remote_copy(
            src_ref=tokens_ref.at[rows_of(block)],
            dst_ref=token_buf.at[owner, block],
            send_sem=m_send.at[step, block],
            recv_sem=m_recv.at[step, block],
            device_id={"tp": mate},
        )

    def x_copy_in(block):
        return pltpu.make_async_remote_copy(
            src_ref=stage.at[block],
            dst_ref=source_ref.at[slot(0, 1 - side), block],
            send_sem=x_send.at[block],
            recv_sem=x_recv.at[block],
            device_id={"ctx": beside},
        )

    def relay(block, lag):
        if lag == 1:
            x_copy_in(block).wait_recv()
            for way in ways:

                @pl.when(half_sent(way, 1))
                def _(way=way):
                    half_copy(block, way, 1).start()

        for way in ways:
            if lag <= hops:

                @pl.when(full_due(way, lag))
                def _(way=way):
                    full_copy(block, way, lag).wait_recv()

                if lag < hops:

                    @pl.when(full_sent(way, lag + 1))
                    def _(way=way):
                        full_copy(block, way, lag + 1).start()

                @pl.when(k_sent(way, lag))
                def _(way=way):
                    k_copy(block, way, lag).start()

            if lag > 1:

                @pl.when(half_due(way, lag - 1))
                def _(way=way):
                    half_copy(block, way, lag - 1).wait_recv()

                if lag <= hops:

                    @pl.when(half_sent(way, lag))
                    def _(way=way):
                        half_copy(block, way, lag).start()

    def step_of(step, carry):
        @pl.when(step < blocks)
        def _():
            make(step)

        for lag in range(1, hops + 2):

            @pl.when((step >= lag) & (step - lag < blocks))
            def _(lag=lag):
                relay(step - lag, lag)

        @pl.when(step == 0)
        def _():
            weight_copies[2].wait()

        @pl.when(step < blocks)
        def _():
            width = query_ref.shape[1]
            wide = min(512, width)
            for start in range(0, width, wide):
                lanes = slice(start, start + wide)
                query_ref[rows_of(step), lanes] = multiply(step, query_weight, lanes)

        return carry

    lax.fori_loop(0, blocks + hops + 1, step_of, 0)

    def drain(block, carry):
        for step in range(1, across):
            y_copy(block, step).wait_send()
        for step in range(across):
            m_copy(block, step).wait_send()
        store(block).wait()
        x_copy(block).wait_send()
        for way in ways:
            for hop in range(1, hops + 1):

                @pl.when(k_due(way, hop))
                def _(way=way, hop=hop):
                    k_received(block, way, hop).wait_recv()

                @pl.when(full_sent(way, hop))
                def _(way=way, hop=hop):
                    full_copy(block, way, hop).wait_send()

                @pl.when(half_sent(way, hop))
                def _(way=way, hop=hop):
                    half_copy(block, way, hop).wait_send()

                @pl.when(k_sent(way, hop))
                def _(way=way, hop=hop):
                    k_copy(block, way, hop).wait_send()

        return carry

    lax.fori_loop(0, blocks, drain, 0)


def gather(tokens, query_weight, key_weight, value_weight):
    tp, ctx = lax.axis_size("tp"), lax.axis_size("ctx")
    across = tp // CORES
    hops = (REACH + 1) // 2
    row_count, depth = tokens.shape
    blocks = row_count // BLOCK
    query_width, key_width = query_weight.shape[1], key_weight.shape[1]
    slots = (2 * hops + 1) * 2
    dma = pltpu.SemaphoreType.DMA
    return pl.pallas_call(
        functools.partial(gather_kernel, tp, ctx, hops),
        out_shape=(
            jax.ShapeDtypeStruct((row_count, query_width), BF16),
            jax.ShapeDtypeStruct((slots, blocks, 2, BLOCK, key_width), BF16),
        ),
        in_specs=[ANY] * 4,
        out_specs=(VMEM, ANY),
        scratch_shapes=[
            pltpu.VMEM((tp, blocks, BLOCK, depth), BF16),
            pltpu.VMEM(query_weight.shape, BF16),
            pltpu.VMEM(key_weight.shape, BF16),
            pltpu.VMEM(value_weight.shape, BF16),
            pltpu.VMEM((blocks, 2, BLOCK, key_width), BF16),
            dma((blocks,)),
            dma((3,)),
            dma((blocks,)),
            dma((max(across - 1, 1), blocks)),
            dma((max(across - 1, 1), blocks)),
            dma((across, blocks)),
            dma((across, blocks)),
            dma((blocks,)),
            dma((blocks,)),
            dma((2, hops, blocks)),
            dma((2, hops, blocks)),
            dma((2, hops, blocks)),
            dma((2, hops, blocks)),
            dma((2, hops, blocks)),
            dma((2, hops, blocks)),
        ],
        compiler_params=pltpu.CompilerParams(
            collective_id=0, has_side_effects=True, vmem_limit_bytes=GRANT
        ),
        cost_estimate=pl.CostEstimate(
            flops=2 * row_count * depth * tp * (query_width + 2 * key_width),
            bytes_accessed=1 << 24,
            transcendentals=0,
        ),
    )(tokens, query_weight, key_weight, value_weight)


def local(tokens, query_weight, key_weight, value_weight, out_weight, links, counts, doc_ids):
    blocks = tokens.shape[0] // BLOCK
    query, source = gather(tokens, query_weight, key_weight, value_weight)
    source = source.reshape((-1,) + source.shape[2:])
    position = lax.axis_index("ctx")
    anchor = (lax.div(position, 2) - (REACH + 1) // 2) * 2 * blocks
    place = jnp.stack([position * blocks, anchor]).astype(jnp.int32)
    attended = attend(place, links, counts, doc_ids, query, source)
    return project(attended, out_weight)


def solution(mesh):
    placed = (
        P("ctx", "tp"),
        P(None, "tp"),
        P(None, "tp"),
        P(None, "tp"),
        P("tp", None),
        P("ctx", None),
        P("ctx"),
        P(),
    )
    return jax.shard_map(
        local, mesh=mesh, in_specs=placed, out_specs=P(("ctx", "tp"), None), check_vma=False
    )
```

```python
import functools

import jax
import jax.numpy as jnp
from jax import lax
from jax.experimental import pallas as pl
from jax.experimental.pallas import tpu as pltpu
from jax.sharding import PartitionSpec as P

HEAD_DIM = 128
BLOCK = 128
LINKS = 16
REACH = 4
CORES = 2
BF16 = jnp.bfloat16
F32 = jnp.float32
VMEM = pl.BlockSpec(memory_space=pltpu.VMEM)
SMEM = pl.BlockSpec(memory_space=pltpu.SMEM)
ANY = pl.BlockSpec(memory_space=pl.ANY)
GRANT = 56 * 1024 * 1024


def gather_kernel(
    tp, ctx, hops, tokens_ref, query_weight_ref, key_weight_ref, value_weight_ref,
    query_ref, source_ref, token_buf, query_weight, key_weight, value_weight, stage,
    load_sems, weight_sems, store_sems, y_send, y_recv, m_send, m_recv,
    x_send, x_recv, full_send, full_recv, half_send, half_recv, k_send, k_recv
):
    blocks = tokens_ref.shape[0] // BLOCK
    across = tp // CORES
    depth = tokens_ref.shape[1]
    pairs = ctx // 2
    me = lax.axis_index("tp")
    chip, core = lax.div(me, CORES), lax.rem(me, CORES)
    mate = chip * CORES + 1 - core
    here = lax.axis_index("ctx")
    pair, side = lax.div(here, 2), lax.rem(here, 2)
    beside = pair * 2 + 1 - side
    ways = (1, -1)

    def exists(offset):
        return (pair + offset >= 0) & (pair + offset < pairs)

    def needed(offset, holder, reader):
        distance = 2 * offset + holder - reader
        return (distance <= REACH) & (distance >= -REACH)

    def slot(offset, holder):
        return (offset + hops) * 2 + holder

    def peer(step):
        return lax.rem(chip + step, across) * CORES + core

    def rows_of(block):
        return pl.ds(pl.multiple_of(block * BLOCK, BLOCK), BLOCK)

    def load(block):
        return pltpu.make_async_copy(
            tokens_ref.at[rows_of(block)], token_buf.at[me, block], load_sems.at[block]
        )

    def y_copy(block, step):
        return pltpu.make_async_remote_copy(
            src_ref=tokens_ref.at[rows_of(block)],
            dst_ref=token_buf.at[me, block],
            send_sem=y_send.at[step - 1, block],
            recv_sem=y_recv.at[step - 1, block],
            device_id={"tp": peer(step)},
        )

    def m_copy(block, step):
        owner = peer(across - step)
        if step == 0:
            source, owner = tokens_ref.at[rows_of(block)], me
        else:
            source = token_buf.at[owner, block]
        return pltpu.make_async_remote_copy(
            src_ref=source,
            dst_ref=token_buf.at[owner, block],
            send_sem=m_send.at[step, block],
            recv_sem=m_recv.at[step, block],
            device_id={"tp": mate},
        )

    weight_copies = [
        pltpu.make_async_copy(key_weight_ref, key_weight, weight_sems.at[0]),
        pltpu.make_async_copy(value_weight_ref, value_weight, weight_sems.at[1]),
        pltpu.make_async_copy(query_weight_ref, query_weight, weight_sems.at[2]),
    ]

    def begin(block, carry):
        load(block).start()
        return carry

    lax.fori_loop(0, blocks, begin, 0)
    for copy in weight_copies:
        copy.start()

    barrier = pltpu.get_barrier_semaphore()
    pl.semaphore_signal(barrier, inc=1, device_id={"tp": mate})
    for step in range(1, across):
        pl.semaphore_signal(barrier, inc=1, device_id={"tp": peer(step)})
    pl.semaphore_signal(barrier, inc=1, device_id={"ctx": beside})
    for way in ways:

        @pl.when(exists(way))
        def _(way=way):
            pl.semaphore_signal(barrier, inc=1, device_id={"ctx": here + 2 * way})

    expected = across + 1 + exists(1).astype(jnp.int32) + exists(-1).astype(jnp.int32)
    pl.semaphore_wait(barrier, expected)

    def push(block, carry):
        for step in range(1, across):
            y_copy(block, step).start()
        m_copy(block, 0).start()
        return carry

    lax.fori_loop(0, blocks, push, 0)

    def store(block):
        return pltpu.make_async_copy(
            stage.at[block], source_ref.at[slot(0, side), block], store_sems.at[block]
        )

    def x_copy(block):
        return pltpu.make_async_remote_copy(
            src_ref=stage.at[block],
            dst_ref=source_ref.at[slot(0, side), block],
            send_sem=x_send.at[block],
            recv_sem=x_recv.at[block],
            device_id={"ctx": beside},
        )

    def full_copy(block, way, hop):
        source = stage.at[block] if hop == 1 else source_ref.at[slot(-way * (hop - 1), side), block]
        return pltpu.make_async_remote_copy(
            src_ref=source,
            dst_ref=source_ref.at[slot(-way * hop, side), block],
            send_sem=full_send.at[ways.index(way), hop - 1, block],
            recv_sem=full_recv.at[ways.index(way), hop - 1, block],
            device_id={"ctx": here + 2 * way},
        )

    def half_copy(block, way, hop):
        return pltpu.make_async_remote_copy(
            src_ref=source_ref.at[slot(-way * (hop - 1), 1 - side), block, 1],
            dst_ref=source_ref.at[slot(-way * hop, 1 - side), block, 1],
            send_sem=half_send.at[ways.index(way), hop - 1, block],
            recv_sem=half_recv.at[ways.index(way), hop - 1, block],
            device_id={"ctx": here + 2 * way},
        )

    def k_copy(block, way, hop):
        return pltpu.make_async_remote_copy(
            src_ref=source_ref.at[slot(-way * hop, side), block, 0],
            dst_ref=source_ref.at[slot(-way * hop, side), block, 0],
            send_sem=k_send.at[ways.index(way), hop - 1, block],
            recv_sem=k_recv.at[ways.index(way), hop - 1, block],
            device_id={"ctx": beside},
        )

    def full_sent(way, hop):
        return exists(way) & exists(-way * (hop - 1))

    def full_due(way, hop):
        return exists(-way * hop)

    def half_sent(way, hop):
        return full_sent(way, hop) & needed(-way * hop, 1 - side, side)

    def half_due(way, hop):
        return full_due(way, hop) & needed(-way * hop, 1 - side, side)

    def k_sent(way, hop):
        return full_due(way, hop) & needed(-way * hop, side, 1 - side)

    def k_due(way, hop):
        return full_due(way, hop) & needed(-way * hop, 1 - side, side)

    def k_received(block, way, hop):
        return pltpu.make_async_remote_copy(
            src_ref=source_ref.at[slot(-way * hop, 1 - side), block, 0],
            dst_ref=source_ref.at[slot(-way * hop, 1 - side), block, 0],
            send_sem=k_send.at[ways.index(way), hop - 1, block],
            recv_sem=k_recv.at[ways.index(way), hop - 1, block],
            device_id={"ctx": beside},
        )

    def multiply(block, weight, lanes):
        return sum(
            jnp.dot(
                token_buf[part, block],
                weight[part * depth : (part + 1) * depth, lanes],
                preferred_element_type=F32,
            )
            for part in range(tp)
        ).astype(BF16)

    def make(block):
        for step in range(1, across):
            y_copy_in(block, step).wait_recv()
            m_copy(block, step).start()
        load(block).wait()
        for step in range(across):
            m_copy_in(block, step).wait_recv()

        @pl.when(block == 0)
        def _():
            weight_copies[0].wait()
            weight_copies[1].wait()

        stage[block, 0] = multiply(block, key_weight, slice(None))
        stage[block, 1] = multiply(block, value_weight, slice(None))
        for way in ways:

            @pl.when(full_sent(way, 1))
            def _(way=way):
                full_copy(block, way, 1).start()

        x_copy(block).start()
        store(block).start()

    def y_copy_in(block, step):
        owner = peer(across - step)
        return pltpu.make_async_remote_copy(
            src_ref=tokens_ref.at[rows_of(block)],
            dst_ref=token_buf.at[owner, block],
            send_sem=y_send.at[step - 1, block],
            recv_sem=y_recv.at[step - 1, block],
            device_id={"tp": peer(step)},
        )

    def m_copy_in(block, step):
        owner = lax.rem(chip + across - step, across) * CORES + 1 - core
        return pltpu.make_async_remote_copy(
            src_ref=tokens_ref.at[rows_of(block)],
            dst_ref=token_buf.at[owner, block],
            send_sem=m_send.at[step, block],
            recv_sem=m_recv.at[step, block],
            device_id={"tp": mate},
        )

    def x_copy_in(block):
        return pltpu.make_async_remote_copy(
            src_ref=stage.at[block],
            dst_ref=source_ref.at[slot(0, 1 - side), block],
            send_sem=x_send.at[block],
            recv_sem=x_recv.at[block],
            device_id={"ctx": beside},
        )

    def relay(block, lag):
        if lag == 1:
            x_copy_in(block).wait_recv()
            for way in ways:

                @pl.when(half_sent(way, 1))
                def _(way=way):
                    half_copy(block, way, 1).start()

        for way in ways:
            if lag <= hops:

                @pl.when(full_due(way, lag))
                def _(way=way):
                    full_copy(block, way, lag).wait_recv()

                if lag < hops:

                    @pl.when(full_sent(way, lag + 1))
                    def _(way=way):
                        full_copy(block, way, lag + 1).start()

                @pl.when(k_sent(way, lag))
                def _(way=way):
                    k_copy(block, way, lag).start()

            if lag > 1:

                @pl.when(half_due(way, lag - 1))
                def _(way=way):
                    half_copy(block, way, lag - 1).wait_recv()

                if lag <= hops:

                    @pl.when(half_sent(way, lag))
                    def _(way=way):
                        half_copy(block, way, lag).start()

    def step_of(step, carry):
        @pl.when(step < blocks)
        def _():
            make(step)

        for lag in range(1, hops + 2):

            @pl.when((step >= lag) & (step - lag < blocks))
            def _(lag=lag):
                relay(step - lag, lag)

        @pl.when(step == 0)
        def _():
            weight_copies[2].wait()

        @pl.when(step < blocks)
        def _():
            width = query_ref.shape[1]
            wide = min(512, width)
            for start in range(0, width, wide):
                lanes = slice(start, start + wide)
                query_ref[rows_of(step), lanes] = multiply(step, query_weight, lanes)

        return carry

    lax.fori_loop(0, blocks + hops + 1, step_of, 0)

    def drain(block, carry):
        for step in range(1, across):
            y_copy(block, step).wait_send()
        for step in range(across):
            m_copy(block, step).wait_send()
        store(block).wait()
        x_copy(block).wait_send()
        for way in ways:
            for hop in range(1, hops + 1):

                @pl.when(k_due(way, hop))
                def _(way=way, hop=hop):
                    k_received(block, way, hop).wait_recv()

                @pl.when(full_sent(way, hop))
                def _(way=way, hop=hop):
                    full_copy(block, way, hop).wait_send()

                @pl.when(half_sent(way, hop))
                def _(way=way, hop=hop):
                    half_copy(block, way, hop).wait_send()

                @pl.when(k_sent(way, hop))
                def _(way=way, hop=hop):
                    k_copy(block, way, hop).wait_send()

        return carry

    lax.fori_loop(0, blocks, drain, 0)


def gather(tokens, query_weight, key_weight, value_weight):
    tp, ctx = lax.axis_size("tp"), lax.axis_size("ctx")
    across = tp // CORES
    hops = (REACH + 1) // 2
    row_count, depth = tokens.shape
    blocks = row_count // BLOCK
    query_width, key_width = query_weight.shape[1], key_weight.shape[1]
    slots = (2 * hops + 1) * 2
    dma = pltpu.SemaphoreType.DMA
    return pl.pallas_call(
        functools.partial(gather_kernel, tp, ctx, hops),
        out_shape=(
            jax.ShapeDtypeStruct((row_count, query_width), BF16),
            jax.ShapeDtypeStruct((slots, blocks, 2, BLOCK, key_width), BF16),
        ),
        in_specs=[ANY] * 4,
        out_specs=(VMEM, ANY),
        scratch_shapes=[
            pltpu.VMEM((tp, blocks, BLOCK, depth), BF16),
            pltpu.VMEM(query_weight.shape, BF16),
            pltpu.VMEM(key_weight.shape, BF16),
            pltpu.VMEM(value_weight.shape, BF16),
            pltpu.VMEM((blocks, 2, BLOCK, key_width), BF16),
            dma((blocks,)),
            dma((3,)),
            dma((blocks,)),
            dma((max(across - 1, 1), blocks)),
            dma((max(across - 1, 1), blocks)),
            dma((across, blocks)),
            dma((across, blocks)),
            dma((blocks,)),
            dma((blocks,)),
            dma((2, hops, blocks)),
            dma((2, hops, blocks)),
            dma((2, hops, blocks)),
            dma((2, hops, blocks)),
            dma((2, hops, blocks)),
            dma((2, hops, blocks)),
        ],
        compiler_params=pltpu.CompilerParams(
            collective_id=0, has_side_effects=True, vmem_limit_bytes=GRANT
        ),
        cost_estimate=pl.CostEstimate(
            flops=2 * row_count * depth * tp * (query_width + 2 * key_width),
            bytes_accessed=1 << 24,
            transcendentals=0,
        ),
    )(tokens, query_weight, key_weight, value_weight)


def finish_kernel(
    tp, chunks, wide, group, hops, links_ref, counts_ref, docs_ref, query_ref, source_ref,
    weight_ref, out_ref, source_buf, weight_buf, score_buf, attended, part_buf, own_buf,
    mate_send, mate_recv, far_send, far_recv, source_sem, weight_sems, mate_send_sems,
    mate_recv_sems, far_send_sems, far_recv_sems
):
    row_count = query_ref.shape[0]
    blocks = row_count // BLOCK
    kv_heads = source_ref.shape[3] // HEAD_DIM
    rows = row_count // tp
    tall = rows * CORES
    across = tp // CORES
    me = lax.axis_index("tp")
    chip, core = lax.div(me, CORES), lax.rem(me, CORES)
    mate = chip * CORES + 1 - core
    here = lax.axis_index("ctx")
    first = here * blocks
    anchor = (lax.div(here, 2) - hops) * 2 * blocks

    source_copy = pltpu.make_async_copy(source_ref, source_buf, source_sem.at[0])
    source_copy.start()

    def weight_copy(index):
        columns = pl.ds(pl.multiple_of(index * wide, wide), wide)
        return pltpu.make_async_copy(
            weight_ref.at[:, columns], weight_buf.at[index], weight_sems.at[index]
        )

    def start_weight(index, carry):
        weight_copy(index).start()
        return carry

    lax.fori_loop(0, chunks, start_weight, 0)

    barrier = pltpu.get_barrier_semaphore()
    pl.semaphore_signal(barrier, inc=1, device_id={"tp": mate})
    for step in range(1, across):
        other = lax.rem(chip + step, across) * CORES + core
        pl.semaphore_signal(barrier, inc=1, device_id={"tp": other})
    pl.semaphore_wait(barrier, across)
    source_copy.wait()

    scale = HEAD_DIM ** (-0.5) * 1.4426950408889634
    pair = 2 * BLOCK
    height = group * BLOCK
    token = lax.rem(lax.broadcasted_iota(jnp.int32, (height, pair), 0), BLOCK)
    column = lax.broadcasted_iota(jnp.int32, (height, pair), 1)
    row_column = lax.broadcasted_iota(jnp.int32, (1, pair), 1)

    def attend(block):
        mine = first + block
        doc = docs_ref[mine]
        live = counts_ref[block]
        places, biases = [], []
        for slot in range(LINKS):
            listed = links_ref[block, slot]
            seen = (slot < live) & ((listed <= mine) | (docs_ref[listed] != doc))
            places.append(jnp.clip(listed - anchor, 0, source_ref.shape[0] - 1))
            biases.append(jnp.where(seen, 0.0, -1e30))
        at = pl.ds(pl.multiple_of(block * BLOCK, BLOCK), BLOCK)

        def of_head(head, carry):
            lanes = pl.ds(pl.multiple_of(head * HEAD_DIM, HEAD_DIM), HEAD_DIM)

            def lanes_of(member):
                start = pl.multiple_of((head * group + member) * HEAD_DIM, HEAD_DIM)
                return pl.ds(start, HEAD_DIM)

            def two(index, kind):
                return jnp.concatenate(
                    [source_buf[places[2 * index + i], kind, :, lanes] for i in range(2)], axis=0
                )

            query = jnp.concatenate(
                [query_ref[at, lanes_of(member)] for member in range(group)], axis=0
            )
            top = None
            for index in range(LINKS // 2):
                scores = lax.dot_general(
                    query, two(index, 0), (((1,), (1,)), ((), ())), preferred_element_type=F32
                )
                bias = jnp.where(row_column < BLOCK, biases[2 * index], biases[2 * index + 1])
                scores = scores * scale + bias
                if index == 0:
                    scores = jnp.where((column >= BLOCK) | (column <= token), scores, -1e30)
                score_buf[index] = scores
                both = jnp.maximum(scores[:, :BLOCK], scores[:, BLOCK:])
                top = both if top is None else jnp.maximum(top, both)
            top = jnp.max(top, axis=1, keepdims=True)
            total, result = None, None
            for index in range(LINKS // 2):
                powers = jnp.exp2(score_buf[index] - top)
                both = powers[:, :BLOCK] + powers[:, BLOCK:]
                total = both if total is None else total + both
                term = jnp.dot(powers.astype(BF16), two(index, 1), preferred_element_type=F32)
                result = term if result is None else result + term
            total = jnp.sum(total, axis=1, keepdims=True)
            result = (result / total).astype(BF16)
            for member in range(group):
                attended[at, lanes_of(member)] = result[member * BLOCK : (member + 1) * BLOCK]
            return carry

        lax.fori_loop(0, kv_heads, of_head, 0)

    def mate_copy(index, step):
        return pltpu.make_async_remote_copy(
            src_ref=mate_send.at[index, step],
            dst_ref=mate_recv.at[index, step],
            send_sem=mate_send_sems.at[index, step],
            recv_sem=mate_recv_sems.at[index, step],
            device_id={"tp": mate},
        )

    def far_copy(index, step):
        other = lax.rem(chip + step, across) * CORES + core
        return pltpu.make_async_remote_copy(
            src_ref=far_send.at[index, step - 1],
            dst_ref=far_recv.at[index, step - 1],
            send_sem=far_send_sems.at[index, step - 1],
            recv_sem=far_recv_sems.at[index, step - 1],
            device_id={"tp": other},
        )

    def rows_of(which):
        return pl.ds(pl.multiple_of(which * rows, rows), rows)

    def turn_of(turn, carry):
        step = lax.rem(turn + 1, across)
        target = lax.rem(chip + step, across)
        per_chip = tall // BLOCK

        def attend_one(index, carry):
            attend(target * per_chip + index)
            return carry

        lax.fori_loop(0, per_chip, attend_one, 0)
        at = pl.ds(pl.multiple_of(target * tall, tall), tall)

        def multiply(index):
            @pl.when(turn == 0)
            def _():
                weight_copy(index).wait()

            part_buf[lax.rem(index, 2)] = jnp.dot(
                attended[at], weight_buf[index], preferred_element_type=F32
            )
            mate_send[index, step] = part_buf[lax.rem(index, 2), rows_of(1 - core)].astype(BF16)
            mate_copy(index, step).start()

        def combine(index):
            mate_copy(index, step).wait_recv()
            total = part_buf[lax.rem(index, 2), rows_of(core)] + mate_recv[index, step].astype(F32)

            @pl.when(step == 0)
            def _():
                own_buf[index] = total

            @pl.when(step > 0)
            def _():
                far_send[index, step - 1] = total.astype(BF16)
                far_copy(index, step).start()

        multiply(0)

        def middle(index, carry):
            multiply(index)
            combine(index - 1)
            return carry

        lax.fori_loop(1, chunks, middle, 0)
        combine(chunks - 1)
        return carry

    lax.fori_loop(0, across, turn_of, 0)

    def close(index, carry):
        total = own_buf[index]
        for step in range(1, across):
            far_copy(index, step).wait_recv()
            total = total + far_recv[index, step - 1].astype(F32)
        columns = pl.ds(pl.multiple_of(index * wide, wide), wide)
        out_ref[:, columns] = total.astype(BF16)
        return carry

    lax.fori_loop(0, chunks, close, 0)

    def drain(index, carry):
        for step in range(across):
            mate_copy(index, step).wait_send()
        for step in range(1, across):
            far_copy(index, step).wait_send()
        return carry

    lax.fori_loop(0, chunks, drain, 0)


def finish(links, counts, doc_ids, query, source, out_weight):
    tp = lax.axis_size("tp")
    across = tp // CORES
    hops = (REACH + 1) // 2
    row_count, depth = query.shape
    width = out_weight.shape[1]
    group = depth // source.shape[3]
    rows = row_count // tp
    wide = min(512, width)
    chunks = width // wide
    dma = pltpu.SemaphoreType.DMA
    return pl.pallas_call(
        functools.partial(finish_kernel, tp, chunks, wide, group, hops),
        out_shape=jax.ShapeDtypeStruct((rows, width), BF16),
        in_specs=[SMEM, SMEM, SMEM, VMEM, ANY, ANY],
        out_specs=VMEM,
        scratch_shapes=[
            pltpu.VMEM(source.shape, BF16),
            pltpu.VMEM((chunks, depth, wide), BF16),
            pltpu.VMEM((LINKS // 2, group * BLOCK, 2 * BLOCK), F32),
            pltpu.VMEM((row_count, depth), BF16),
            pltpu.VMEM((2, rows * CORES, wide), F32),
            pltpu.VMEM((chunks, rows, wide), F32),
            pltpu.VMEM((chunks, across, rows, wide), BF16),
            pltpu.VMEM((chunks, across, rows, wide), BF16),
            pltpu.VMEM((chunks, max(across - 1, 1), rows, wide), BF16),
            pltpu.VMEM((chunks, max(across - 1, 1), rows, wide), BF16),
            dma((1,)),
            dma((chunks,)),
            dma((chunks, across)),
            dma((chunks, across)),
            dma((chunks, max(across - 1, 1))),
            dma((chunks, max(across - 1, 1))),
        ],
        compiler_params=pltpu.CompilerParams(
            collective_id=1, has_side_effects=True, vmem_limit_bytes=GRANT
        ),
        cost_estimate=pl.CostEstimate(
            flops=2 * row_count * depth * (width + 2 * LINKS * BLOCK),
            bytes_accessed=1 << 24,
            transcendentals=0,
        ),
    )(links, counts, doc_ids, query, source, out_weight)


def local(tokens, query_weight, key_weight, value_weight, out_weight, links, counts, doc_ids):
    query, source = gather(tokens, query_weight, key_weight, value_weight)
    source = source.reshape((-1,) + source.shape[2:])
    return finish(links, counts, doc_ids, query, source, out_weight)


def solution(mesh):
    placed = (
        P("ctx", "tp"),
        P(None, "tp"),
        P(None, "tp"),
        P(None, "tp"),
        P("tp", None),
        P("ctx", None),
        P("ctx"),
        P(),
    )
    return jax.shard_map(
        local, mesh=mesh, in_specs=placed, out_specs=P(("ctx", "tp"), None), check_vma=False
    )
```

```python
import functools

import jax
import jax.numpy as jnp
from jax import lax
from jax.experimental import pallas as pl
from jax.experimental.pallas import tpu as pltpu
from jax.sharding import PartitionSpec as P

HEAD_DIM = 128
BLOCK = 128
LINKS = 16
REACH = 4
CORES = 2
BF16 = jnp.bfloat16
F32 = jnp.float32
VMEM = pl.BlockSpec(memory_space=pltpu.VMEM)
SMEM = pl.BlockSpec(memory_space=pltpu.SMEM)
ANY = pl.BlockSpec(memory_space=pl.ANY)
GRANT = 56 * 1024 * 1024


def gather_kernel(
    tp, ctx, hops, tokens_ref, query_weight_ref, key_weight_ref, value_weight_ref,
    query_ref, source_ref, token_buf, query_weight, key_weight, value_weight, stage,
    load_sems, weight_sems, store_sems, y_send, y_recv, m_send, m_recv,
    x_send, x_recv, full_send, full_recv, half_send, half_recv, k_send, k_recv
):
    blocks = tokens_ref.shape[0] // BLOCK
    across = tp // CORES
    depth = tokens_ref.shape[1]
    pairs = ctx // 2
    me = lax.axis_index("tp")
    chip, core = lax.div(me, CORES), lax.rem(me, CORES)
    mate = chip * CORES + 1 - core
    here = lax.axis_index("ctx")
    pair, side = lax.div(here, 2), lax.rem(here, 2)
    beside = pair * 2 + 1 - side
    ways = (1, -1)

    def exists(offset):
        return (pair + offset >= 0) & (pair + offset < pairs)

    def needed(offset, holder, reader):
        distance = 2 * offset + holder - reader
        return (distance <= REACH) & (distance >= -REACH)

    def slot(offset, holder):
        return (offset + hops) * 2 + holder

    def peer(step):
        return lax.rem(chip + step, across) * CORES + core

    def rows_of(block):
        return pl.ds(pl.multiple_of(block * BLOCK, BLOCK), BLOCK)

    def load(block):
        return pltpu.make_async_copy(
            tokens_ref.at[rows_of(block)], token_buf.at[me, block], load_sems.at[block]
        )

    def y_copy(block, step):
        return pltpu.make_async_remote_copy(
            src_ref=tokens_ref.at[rows_of(block)],
            dst_ref=token_buf.at[me, block],
            send_sem=y_send.at[step - 1, block],
            recv_sem=y_recv.at[step - 1, block],
            device_id={"tp": peer(step)},
        )

    def m_copy(block, step):
        owner = peer(across - step)
        if step == 0:
            source, owner = tokens_ref.at[rows_of(block)], me
        else:
            source = token_buf.at[owner, block]
        return pltpu.make_async_remote_copy(
            src_ref=source,
            dst_ref=token_buf.at[owner, block],
            send_sem=m_send.at[step, block],
            recv_sem=m_recv.at[step, block],
            device_id={"tp": mate},
        )

    weight_copies = [
        pltpu.make_async_copy(key_weight_ref, key_weight, weight_sems.at[0]),
        pltpu.make_async_copy(value_weight_ref, value_weight, weight_sems.at[1]),
        pltpu.make_async_copy(query_weight_ref, query_weight, weight_sems.at[2]),
    ]

    def begin(block, carry):
        load(block).start()
        return carry

    lax.fori_loop(0, blocks, begin, 0)
    for copy in weight_copies:
        copy.start()

    barrier = pltpu.get_barrier_semaphore()
    pl.semaphore_signal(barrier, inc=1, device_id={"tp": mate})
    for step in range(1, across):
        pl.semaphore_signal(barrier, inc=1, device_id={"tp": peer(step)})
    pl.semaphore_signal(barrier, inc=1, device_id={"ctx": beside})
    for way in ways:

        @pl.when(exists(way))
        def _(way=way):
            pl.semaphore_signal(barrier, inc=1, device_id={"ctx": here + 2 * way})

    expected = across + 1 + exists(1).astype(jnp.int32) + exists(-1).astype(jnp.int32)
    pl.semaphore_wait(barrier, expected)

    def push(block, carry):
        for step in range(1, across):
            y_copy(block, step).start()
        m_copy(block, 0).start()
        return carry

    lax.fori_loop(0, blocks, push, 0)

    def store(block):
        return pltpu.make_async_copy(
            stage.at[block], source_ref.at[slot(0, side), block], store_sems.at[block]
        )

    def x_copy(block):
        return pltpu.make_async_remote_copy(
            src_ref=stage.at[block],
            dst_ref=source_ref.at[slot(0, side), block],
            send_sem=x_send.at[block],
            recv_sem=x_recv.at[block],
            device_id={"ctx": beside},
        )

    def full_copy(block, way, hop):
        source = stage.at[block] if hop == 1 else source_ref.at[slot(-way * (hop - 1), side), block]
        return pltpu.make_async_remote_copy(
            src_ref=source,
            dst_ref=source_ref.at[slot(-way * hop, side), block],
            send_sem=full_send.at[ways.index(way), hop - 1, block],
            recv_sem=full_recv.at[ways.index(way), hop - 1, block],
            device_id={"ctx": here + 2 * way},
        )

    def half_copy(block, way, hop):
        return pltpu.make_async_remote_copy(
            src_ref=source_ref.at[slot(-way * (hop - 1), 1 - side), block, 1],
            dst_ref=source_ref.at[slot(-way * hop, 1 - side), block, 1],
            send_sem=half_send.at[ways.index(way), hop - 1, block],
            recv_sem=half_recv.at[ways.index(way), hop - 1, block],
            device_id={"ctx": here + 2 * way},
        )

    def k_copy(block, way, hop):
        return pltpu.make_async_remote_copy(
            src_ref=source_ref.at[slot(-way * hop, side), block, 0],
            dst_ref=source_ref.at[slot(-way * hop, side), block, 0],
            send_sem=k_send.at[ways.index(way), hop - 1, block],
            recv_sem=k_recv.at[ways.index(way), hop - 1, block],
            device_id={"ctx": beside},
        )

    def full_sent(way, hop):
        return exists(way) & exists(-way * (hop - 1))

    def full_due(way, hop):
        return exists(-way * hop)

    def half_sent(way, hop):
        return full_sent(way, hop) & needed(-way * hop, 1 - side, side)

    def half_due(way, hop):
        return full_due(way, hop) & needed(-way * hop, 1 - side, side)

    def k_sent(way, hop):
        return full_due(way, hop) & needed(-way * hop, side, 1 - side)

    def k_due(way, hop):
        return full_due(way, hop) & needed(-way * hop, 1 - side, side)

    def k_received(block, way, hop):
        return pltpu.make_async_remote_copy(
            src_ref=source_ref.at[slot(-way * hop, 1 - side), block, 0],
            dst_ref=source_ref.at[slot(-way * hop, 1 - side), block, 0],
            send_sem=k_send.at[ways.index(way), hop - 1, block],
            recv_sem=k_recv.at[ways.index(way), hop - 1, block],
            device_id={"ctx": beside},
        )

    def multiply(block, weight, lanes):
        return sum(
            jnp.dot(
                token_buf[part, block],
                weight[part * depth : (part + 1) * depth, lanes],
                preferred_element_type=F32,
            )
            for part in range(tp)
        ).astype(BF16)

    def make(block):
        for step in range(1, across):
            y_copy_in(block, step).wait_recv()
            m_copy(block, step).start()
        load(block).wait()
        for step in range(across):
            m_copy_in(block, step).wait_recv()

        @pl.when(block == 0)
        def _():
            weight_copies[0].wait()
            weight_copies[1].wait()

        stage[block, 0] = multiply(block, key_weight, slice(None))
        stage[block, 1] = multiply(block, value_weight, slice(None))
        for way in ways:

            @pl.when(full_sent(way, 1))
            def _(way=way):
                full_copy(block, way, 1).start()

        x_copy(block).start()
        store(block).start()

    def y_copy_in(block, step):
        owner = peer(across - step)
        return pltpu.make_async_remote_copy(
            src_ref=tokens_ref.at[rows_of(block)],
            dst_ref=token_buf.at[owner, block],
            send_sem=y_send.at[step - 1, block],
            recv_sem=y_recv.at[step - 1, block],
            device_id={"tp": peer(step)},
        )

    def m_copy_in(block, step):
        owner = lax.rem(chip + across - step, across) * CORES + 1 - core
        return pltpu.make_async_remote_copy(
            src_ref=tokens_ref.at[rows_of(block)],
            dst_ref=token_buf.at[owner, block],
            send_sem=m_send.at[step, block],
            recv_sem=m_recv.at[step, block],
            device_id={"tp": mate},
        )

    def x_copy_in(block):
        return pltpu.make_async_remote_copy(
            src_ref=stage.at[block],
            dst_ref=source_ref.at[slot(0, 1 - side), block],
            send_sem=x_send.at[block],
            recv_sem=x_recv.at[block],
            device_id={"ctx": beside},
        )

    def relay(block, lag):
        if lag == 1:
            x_copy_in(block).wait_recv()
            for way in ways:

                @pl.when(half_sent(way, 1))
                def _(way=way):
                    half_copy(block, way, 1).start()

        for way in ways:
            if lag <= hops:

                @pl.when(full_due(way, lag))
                def _(way=way):
                    full_copy(block, way, lag).wait_recv()

                if lag < hops:

                    @pl.when(full_sent(way, lag + 1))
                    def _(way=way):
                        full_copy(block, way, lag + 1).start()

                @pl.when(k_sent(way, lag))
                def _(way=way):
                    k_copy(block, way, lag).start()

            if lag > 1:

                @pl.when(half_due(way, lag - 1))
                def _(way=way):
                    half_copy(block, way, lag - 1).wait_recv()

                if lag <= hops:

                    @pl.when(half_sent(way, lag))
                    def _(way=way):
                        half_copy(block, way, lag).start()

    def step_of(step, carry):
        @pl.when(step < blocks)
        def _():
            make(step)

        for lag in range(1, hops + 2):

            @pl.when((step >= lag) & (step - lag < blocks))
            def _(lag=lag):
                relay(step - lag, lag)

        @pl.when(step == 0)
        def _():
            weight_copies[2].wait()

        @pl.when(step < blocks)
        def _():
            width = query_ref.shape[1]
            wide = min(512, width)
            for start in range(0, width, wide):
                lanes = slice(start, start + wide)
                query_ref[rows_of(step), lanes] = multiply(step, query_weight, lanes)

        return carry

    lax.fori_loop(0, blocks + hops + 1, step_of, 0)

    def drain(block, carry):
        for step in range(1, across):
            y_copy(block, step).wait_send()
        for step in range(across):
            m_copy(block, step).wait_send()
        store(block).wait()
        x_copy(block).wait_send()
        for way in ways:
            for hop in range(1, hops + 1):

                @pl.when(k_due(way, hop))
                def _(way=way, hop=hop):
                    k_received(block, way, hop).wait_recv()

                @pl.when(full_sent(way, hop))
                def _(way=way, hop=hop):
                    full_copy(block, way, hop).wait_send()

                @pl.when(half_sent(way, hop))
                def _(way=way, hop=hop):
                    half_copy(block, way, hop).wait_send()

                @pl.when(k_sent(way, hop))
                def _(way=way, hop=hop):
                    k_copy(block, way, hop).wait_send()

        return carry

    lax.fori_loop(0, blocks, drain, 0)


def gather(tokens, query_weight, key_weight, value_weight):
    tp, ctx = lax.axis_size("tp"), lax.axis_size("ctx")
    across = tp // CORES
    hops = (REACH + 1) // 2
    row_count, depth = tokens.shape
    blocks = row_count // BLOCK
    query_width, key_width = query_weight.shape[1], key_weight.shape[1]
    slots = (2 * hops + 1) * 2
    dma = pltpu.SemaphoreType.DMA
    return pl.pallas_call(
        functools.partial(gather_kernel, tp, ctx, hops),
        out_shape=(
            jax.ShapeDtypeStruct((row_count, query_width), BF16),
            jax.ShapeDtypeStruct((slots, blocks, 2, BLOCK, key_width), BF16),
        ),
        in_specs=[ANY] * 4,
        out_specs=(VMEM, ANY),
        scratch_shapes=[
            pltpu.VMEM((tp, blocks, BLOCK, depth), BF16),
            pltpu.VMEM(query_weight.shape, BF16),
            pltpu.VMEM(key_weight.shape, BF16),
            pltpu.VMEM(value_weight.shape, BF16),
            pltpu.VMEM((blocks, 2, BLOCK, key_width), BF16),
            dma((blocks,)),
            dma((3,)),
            dma((blocks,)),
            dma((max(across - 1, 1), blocks)),
            dma((max(across - 1, 1), blocks)),
            dma((across, blocks)),
            dma((across, blocks)),
            dma((blocks,)),
            dma((blocks,)),
            dma((2, hops, blocks)),
            dma((2, hops, blocks)),
            dma((2, hops, blocks)),
            dma((2, hops, blocks)),
            dma((2, hops, blocks)),
            dma((2, hops, blocks)),
        ],
        compiler_params=pltpu.CompilerParams(
            collective_id=0, has_side_effects=True, vmem_limit_bytes=GRANT
        ),
        cost_estimate=pl.CostEstimate(
            flops=2 * row_count * depth * tp * (query_width + 2 * key_width),
            bytes_accessed=1 << 24,
            transcendentals=0,
        ),
    )(tokens, query_weight, key_weight, value_weight)


def finish_kernel(
    tp, chunks, wide, group, hops, links_ref, counts_ref, docs_ref, query_ref, source_ref,
    weight_ref, out_ref, source_buf, weight_buf, score_buf, attended, part_buf, own_buf,
    mate_send, mate_recv, far_send, far_recv, source_sem, weight_sems, mate_send_sems,
    mate_recv_sems, far_send_sems, far_recv_sems
):
    row_count = query_ref.shape[0]
    blocks = row_count // BLOCK
    kv_heads = source_ref.shape[3] // HEAD_DIM
    rows = row_count // tp
    tall = rows * CORES
    across = tp // CORES
    me = lax.axis_index("tp")
    chip, core = lax.div(me, CORES), lax.rem(me, CORES)
    mate = chip * CORES + 1 - core
    here = lax.axis_index("ctx")
    first = here * blocks
    anchor = (lax.div(here, 2) - hops) * 2 * blocks

    source_copy = pltpu.make_async_copy(source_ref, source_buf, source_sem.at[0])
    source_copy.start()

    def weight_copy(index):
        columns = pl.ds(pl.multiple_of(index * wide, wide), wide)
        return pltpu.make_async_copy(
            weight_ref.at[:, columns], weight_buf.at[index], weight_sems.at[index]
        )

    def start_weight(index, carry):
        weight_copy(index).start()
        return carry

    lax.fori_loop(0, chunks, start_weight, 0)

    barrier = pltpu.get_barrier_semaphore()
    pl.semaphore_signal(barrier, inc=1, device_id={"tp": mate})
    for step in range(1, across):
        other = lax.rem(chip + step, across) * CORES + core
        pl.semaphore_signal(barrier, inc=1, device_id={"tp": other})
    pl.semaphore_wait(barrier, across)
    source_copy.wait()

    scale = HEAD_DIM ** (-0.5) * 1.4426950408889634
    pair = 2 * BLOCK
    height = group * BLOCK
    token = lax.rem(lax.broadcasted_iota(jnp.int32, (height, pair), 0), BLOCK)
    column = lax.broadcasted_iota(jnp.int32, (height, pair), 1)
    row_column = lax.broadcasted_iota(jnp.int32, (1, pair), 1)

    def attend(block):
        mine = first + block
        doc = docs_ref[mine]
        live = counts_ref[block]
        places, biases = [], []
        for slot in range(LINKS):
            listed = links_ref[block, slot]
            seen = (slot < live) & ((listed <= mine) | (docs_ref[listed] != doc))
            places.append(jnp.clip(listed - anchor, 0, source_ref.shape[0] - 1))
            biases.append(jnp.where(seen, 0.0, -1e30))
        at = pl.ds(pl.multiple_of(block * BLOCK, BLOCK), BLOCK)

        def lanes_of(member):
            return slice(member * HEAD_DIM, (member + 1) * HEAD_DIM)

        def two(index, kind, head):
            return jnp.concatenate(
                [
                    source_buf[places[2 * index + i], kind, :, lanes_of(head)]
                    for i in range(2)
                ],
                axis=0,
            )

        def first_pass(query, head, index):
            scores = lax.dot_general(
                query, two(index, 0, head), (((1,), (1,)), ((), ())), preferred_element_type=F32
            )
            bias = jnp.where(row_column < BLOCK, biases[2 * index], biases[2 * index + 1])
            scores = scores * scale + bias
            if index == 0:
                scores = jnp.where((column >= BLOCK) | (column <= token), scores, -1e30)
            score_buf[head % 2, index] = scores
            return jnp.maximum(scores[:, :BLOCK], scores[:, BLOCK:])

        def second_pass(top, head, index):
            powers = jnp.exp2(score_buf[head % 2, index] - top)
            term = jnp.dot(powers.astype(BF16), two(index, 1, head), preferred_element_type=F32)
            return powers[:, :BLOCK] + powers[:, BLOCK:], term

        top = None
        for head in range(kv_heads + 1):
            best, total, result = None, None, None
            if head < kv_heads:
                query = jnp.concatenate(
                    [query_ref[at, lanes_of(head * group + member)] for member in range(group)],
                    axis=0,
                )
            for index in range(LINKS // 2):
                if head < kv_heads:
                    both = first_pass(query, head, index)
                    best = both if best is None else jnp.maximum(best, both)
                if head > 0:
                    both, term = second_pass(top, head - 1, index)
                    total = both if total is None else total + both
                    result = term if result is None else result + term
            if head > 0:
                result = (result / jnp.sum(total, axis=1, keepdims=True)).astype(BF16)
                for member in range(group):
                    attended[at, lanes_of((head - 1) * group + member)] = result[
                        member * BLOCK : (member + 1) * BLOCK
                    ]
            if head < kv_heads:
                top = jnp.max(best, axis=1, keepdims=True)

    def mate_copy(index, step):
        return pltpu.make_async_remote_copy(
            src_ref=mate_send.at[index, step],
            dst_ref=mate_recv.at[index, step],
            send_sem=mate_send_sems.at[index, step],
            recv_sem=mate_recv_sems.at[index, step],
            device_id={"tp": mate},
        )

    def far_copy(index, step):
        other = lax.rem(chip + step, across) * CORES + core
        return pltpu.make_async_remote_copy(
            src_ref=far_send.at[index, step - 1],
            dst_ref=far_recv.at[index, step - 1],
            send_sem=far_send_sems.at[index, step - 1],
            recv_sem=far_recv_sems.at[index, step - 1],
            device_id={"tp": other},
        )

    def rows_of(which):
        return pl.ds(pl.multiple_of(which * rows, rows), rows)

    def turn_of(turn, carry):
        step = lax.rem(turn + 1, across)
        target = lax.rem(chip + step, across)
        per_chip = tall // BLOCK

        def attend_one(index, carry):
            attend(target * per_chip + index)
            return carry

        lax.fori_loop(0, per_chip, attend_one, 0)
        at = pl.ds(pl.multiple_of(target * tall, tall), tall)

        def multiply(index):
            @pl.when(turn == 0)
            def _():
                weight_copy(index).wait()

            part_buf[lax.rem(index, 2)] = jnp.dot(
                attended[at], weight_buf[index], preferred_element_type=F32
            )
            mate_send[index, step] = part_buf[lax.rem(index, 2), rows_of(1 - core)].astype(BF16)
            mate_copy(index, step).start()

        def combine(index):
            mate_copy(index, step).wait_recv()
            total = part_buf[lax.rem(index, 2), rows_of(core)] + mate_recv[index, step].astype(F32)

            @pl.when(step == 0)
            def _():
                own_buf[index] = total

            @pl.when(step > 0)
            def _():
                far_send[index, step - 1] = total.astype(BF16)
                far_copy(index, step).start()

        multiply(0)

        def middle(index, carry):
            multiply(index)
            combine(index - 1)
            return carry

        lax.fori_loop(1, chunks, middle, 0)
        combine(chunks - 1)
        return carry

    lax.fori_loop(0, across, turn_of, 0)

    def close(index, carry):
        total = own_buf[index]
        for step in range(1, across):
            far_copy(index, step).wait_recv()
            total = total + far_recv[index, step - 1].astype(F32)
        columns = pl.ds(pl.multiple_of(index * wide, wide), wide)
        out_ref[:, columns] = total.astype(BF16)
        return carry

    lax.fori_loop(0, chunks, close, 0)

    def drain(index, carry):
        for step in range(across):
            mate_copy(index, step).wait_send()
        for step in range(1, across):
            far_copy(index, step).wait_send()
        return carry

    lax.fori_loop(0, chunks, drain, 0)


def finish(links, counts, doc_ids, query, source, out_weight):
    tp = lax.axis_size("tp")
    across = tp // CORES
    hops = (REACH + 1) // 2
    row_count, depth = query.shape
    width = out_weight.shape[1]
    group = depth // source.shape[3]
    rows = row_count // tp
    wide = min(512, width)
    chunks = width // wide
    dma = pltpu.SemaphoreType.DMA
    return pl.pallas_call(
        functools.partial(finish_kernel, tp, chunks, wide, group, hops),
        out_shape=jax.ShapeDtypeStruct((rows, width), BF16),
        in_specs=[SMEM, SMEM, SMEM, VMEM, ANY, ANY],
        out_specs=VMEM,
        scratch_shapes=[
            pltpu.VMEM(source.shape, BF16),
            pltpu.VMEM((chunks, depth, wide), BF16),
            pltpu.VMEM((2, LINKS // 2, group * BLOCK, 2 * BLOCK), F32),
            pltpu.VMEM((row_count, depth), BF16),
            pltpu.VMEM((2, rows * CORES, wide), F32),
            pltpu.VMEM((chunks, rows, wide), F32),
            pltpu.VMEM((chunks, across, rows, wide), BF16),
            pltpu.VMEM((chunks, across, rows, wide), BF16),
            pltpu.VMEM((chunks, max(across - 1, 1), rows, wide), BF16),
            pltpu.VMEM((chunks, max(across - 1, 1), rows, wide), BF16),
            dma((1,)),
            dma((chunks,)),
            dma((chunks, across)),
            dma((chunks, across)),
            dma((chunks, max(across - 1, 1))),
            dma((chunks, max(across - 1, 1))),
        ],
        compiler_params=pltpu.CompilerParams(
            collective_id=1, has_side_effects=True, vmem_limit_bytes=GRANT
        ),
        cost_estimate=pl.CostEstimate(
            flops=2 * row_count * depth * (width + 2 * LINKS * BLOCK),
            bytes_accessed=1 << 24,
            transcendentals=0,
        ),
    )(links, counts, doc_ids, query, source, out_weight)


def local(tokens, query_weight, key_weight, value_weight, out_weight, links, counts, doc_ids):
    query, source = gather(tokens, query_weight, key_weight, value_weight)
    source = source.reshape((-1,) + source.shape[2:])
    return finish(links, counts, doc_ids, query, source, out_weight)


def solution(mesh):
    placed = (
        P("ctx", "tp"),
        P(None, "tp"),
        P(None, "tp"),
        P(None, "tp"),
        P("tp", None),
        P("ctx", None),
        P("ctx"),
        P(),
    )
    return jax.shard_map(
        local, mesh=mesh, in_specs=placed, out_specs=P(("ctx", "tp"), None), check_vma=False
    )
```

```python
import functools

import jax
import jax.numpy as jnp
from jax import lax
from jax.experimental import pallas as pl
from jax.experimental.pallas import tpu as pltpu
from jax.sharding import PartitionSpec as P

HEAD_DIM = 128
BLOCK = 128
LINKS = 16
REACH = 4
CORES = 2
BF16 = jnp.bfloat16
F32 = jnp.float32
VMEM = pl.BlockSpec(memory_space=pltpu.VMEM)
SMEM = pl.BlockSpec(memory_space=pltpu.SMEM)
ANY = pl.BlockSpec(memory_space=pl.ANY)
GRANT = 56 * 1024 * 1024


def gather_kernel(
    tp, ctx, hops, tokens_ref, query_weight_ref, key_weight_ref, value_weight_ref,
    query_ref, source_ref, token_buf, query_weight, key_weight, value_weight, stage,
    load_sems, weight_sems, store_sems, y_send, y_recv, m_send, m_recv,
    x_send, x_recv, full_send, full_recv, half_send, half_recv, k_send, k_recv
):
    blocks = tokens_ref.shape[0] // BLOCK
    across = tp // CORES
    depth = tokens_ref.shape[1]
    pairs = ctx // 2
    me = lax.axis_index("tp")
    chip, core = lax.div(me, CORES), lax.rem(me, CORES)
    mate = chip * CORES + 1 - core
    here = lax.axis_index("ctx")
    pair, side = lax.div(here, 2), lax.rem(here, 2)
    beside = pair * 2 + 1 - side
    ways = (1, -1)

    def exists(offset):
        return (pair + offset >= 0) & (pair + offset < pairs)

    def needed(offset, holder, reader):
        distance = 2 * offset + holder - reader
        return (distance <= REACH) & (distance >= -REACH)

    def slot(offset, holder):
        return (offset + hops) * 2 + holder

    def peer(step):
        return lax.rem(chip + step, across) * CORES + core

    def rows_of(block):
        return pl.ds(pl.multiple_of(block * BLOCK, BLOCK), BLOCK)

    def load(block):
        return pltpu.make_async_copy(
            tokens_ref.at[rows_of(block)], token_buf.at[me, block], load_sems.at[block]
        )

    def y_copy(block, step):
        return pltpu.make_async_remote_copy(
            src_ref=tokens_ref.at[rows_of(block)],
            dst_ref=token_buf.at[me, block],
            send_sem=y_send.at[step - 1, block],
            recv_sem=y_recv.at[step - 1, block],
            device_id={"tp": peer(step)},
        )

    def m_copy(block, step):
        owner = peer(across - step)
        if step == 0:
            source, owner = tokens_ref.at[rows_of(block)], me
        else:
            source = token_buf.at[owner, block]
        return pltpu.make_async_remote_copy(
            src_ref=source,
            dst_ref=token_buf.at[owner, block],
            send_sem=m_send.at[step, block],
            recv_sem=m_recv.at[step, block],
            device_id={"tp": mate},
        )

    weight_copies = [
        pltpu.make_async_copy(key_weight_ref, key_weight, weight_sems.at[0]),
        pltpu.make_async_copy(value_weight_ref, value_weight, weight_sems.at[1]),
        pltpu.make_async_copy(query_weight_ref, query_weight, weight_sems.at[2]),
    ]

    def begin(block, carry):
        load(block).start()
        return carry

    lax.fori_loop(0, blocks, begin, 0)
    for copy in weight_copies:
        copy.start()

    barrier = pltpu.get_barrier_semaphore()
    pl.semaphore_signal(barrier, inc=1, device_id={"tp": mate})
    for step in range(1, across):
        pl.semaphore_signal(barrier, inc=1, device_id={"tp": peer(step)})
    pl.semaphore_signal(barrier, inc=1, device_id={"ctx": beside})
    for way in ways:

        @pl.when(exists(way))
        def _(way=way):
            pl.semaphore_signal(barrier, inc=1, device_id={"ctx": here + 2 * way})

    expected = across + 1 + exists(1).astype(jnp.int32) + exists(-1).astype(jnp.int32)
    pl.semaphore_wait(barrier, expected)

    def push(block, carry):
        for step in range(1, across):
            y_copy(block, step).start()
        m_copy(block, 0).start()
        return carry

    lax.fori_loop(0, blocks, push, 0)

    def store(block):
        return pltpu.make_async_copy(
            stage.at[block], source_ref.at[slot(0, side), block], store_sems.at[block]
        )

    def x_copy(block):
        return pltpu.make_async_remote_copy(
            src_ref=stage.at[block],
            dst_ref=source_ref.at[slot(0, side), block],
            send_sem=x_send.at[block],
            recv_sem=x_recv.at[block],
            device_id={"ctx": beside},
        )

    def full_copy(block, way, hop):
        source = stage.at[block] if hop == 1 else source_ref.at[slot(-way * (hop - 1), side), block]
        return pltpu.make_async_remote_copy(
            src_ref=source,
            dst_ref=source_ref.at[slot(-way * hop, side), block],
            send_sem=full_send.at[ways.index(way), hop - 1, block],
            recv_sem=full_recv.at[ways.index(way), hop - 1, block],
            device_id={"ctx": here + 2 * way},
        )

    def half_copy(block, way, hop):
        return pltpu.make_async_remote_copy(
            src_ref=source_ref.at[slot(-way * (hop - 1), 1 - side), block, 1],
            dst_ref=source_ref.at[slot(-way * hop, 1 - side), block, 1],
            send_sem=half_send.at[ways.index(way), hop - 1, block],
            recv_sem=half_recv.at[ways.index(way), hop - 1, block],
            device_id={"ctx": here + 2 * way},
        )

    def k_copy(block, way, hop):
        return pltpu.make_async_remote_copy(
            src_ref=source_ref.at[slot(-way * hop, side), block, 0],
            dst_ref=source_ref.at[slot(-way * hop, side), block, 0],
            send_sem=k_send.at[ways.index(way), hop - 1, block],
            recv_sem=k_recv.at[ways.index(way), hop - 1, block],
            device_id={"ctx": beside},
        )

    def full_sent(way, hop):
        return exists(way) & exists(-way * (hop - 1))

    def full_due(way, hop):
        return exists(-way * hop)

    def half_sent(way, hop):
        return full_sent(way, hop) & needed(-way * hop, 1 - side, side)

    def half_due(way, hop):
        return full_due(way, hop) & needed(-way * hop, 1 - side, side)

    def k_sent(way, hop):
        return full_due(way, hop) & needed(-way * hop, side, 1 - side)

    def k_due(way, hop):
        return full_due(way, hop) & needed(-way * hop, 1 - side, side)

    def k_received(block, way, hop):
        return pltpu.make_async_remote_copy(
            src_ref=source_ref.at[slot(-way * hop, 1 - side), block, 0],
            dst_ref=source_ref.at[slot(-way * hop, 1 - side), block, 0],
            send_sem=k_send.at[ways.index(way), hop - 1, block],
            recv_sem=k_recv.at[ways.index(way), hop - 1, block],
            device_id={"ctx": beside},
        )

    def multiply(block, weight, lanes):
        return sum(
            jnp.dot(
                token_buf[part, block],
                weight[part * depth : (part + 1) * depth, lanes],
                preferred_element_type=F32,
            )
            for part in range(tp)
        ).astype(BF16)

    def make(block):
        for step in range(1, across):
            y_copy_in(block, step).wait_recv()
            m_copy(block, step).start()
        load(block).wait()
        for step in range(across):
            m_copy_in(block, step).wait_recv()

        @pl.when(block == 0)
        def _():
            weight_copies[0].wait()
            weight_copies[1].wait()

        stage[block, 0] = multiply(block, key_weight, slice(None))
        stage[block, 1] = multiply(block, value_weight, slice(None))
        for way in ways:

            @pl.when(full_sent(way, 1))
            def _(way=way):
                full_copy(block, way, 1).start()

        x_copy(block).start()
        store(block).start()

    def y_copy_in(block, step):
        owner = peer(across - step)
        return pltpu.make_async_remote_copy(
            src_ref=tokens_ref.at[rows_of(block)],
            dst_ref=token_buf.at[owner, block],
            send_sem=y_send.at[step - 1, block],
            recv_sem=y_recv.at[step - 1, block],
            device_id={"tp": peer(step)},
        )

    def m_copy_in(block, step):
        owner = lax.rem(chip + across - step, across) * CORES + 1 - core
        return pltpu.make_async_remote_copy(
            src_ref=tokens_ref.at[rows_of(block)],
            dst_ref=token_buf.at[owner, block],
            send_sem=m_send.at[step, block],
            recv_sem=m_recv.at[step, block],
            device_id={"tp": mate},
        )

    def x_copy_in(block):
        return pltpu.make_async_remote_copy(
            src_ref=stage.at[block],
            dst_ref=source_ref.at[slot(0, 1 - side), block],
            send_sem=x_send.at[block],
            recv_sem=x_recv.at[block],
            device_id={"ctx": beside},
        )

    def relay(block, lag):
        if lag == 1:
            x_copy_in(block).wait_recv()
            for way in ways:

                @pl.when(half_sent(way, 1))
                def _(way=way):
                    half_copy(block, way, 1).start()

        for way in ways:
            if lag <= hops:

                @pl.when(full_due(way, lag))
                def _(way=way):
                    full_copy(block, way, lag).wait_recv()

                if lag < hops:

                    @pl.when(full_sent(way, lag + 1))
                    def _(way=way):
                        full_copy(block, way, lag + 1).start()

                @pl.when(k_sent(way, lag))
                def _(way=way):
                    k_copy(block, way, lag).start()

            if lag > 1:

                @pl.when(half_due(way, lag - 1))
                def _(way=way):
                    half_copy(block, way, lag - 1).wait_recv()

                if lag <= hops:

                    @pl.when(half_sent(way, lag))
                    def _(way=way):
                        half_copy(block, way, lag).start()

    def step_of(step, carry):
        @pl.when(step < blocks)
        def _():
            make(step)

        for lag in range(1, hops + 2):

            @pl.when((step >= lag) & (step - lag < blocks))
            def _(lag=lag):
                relay(step - lag, lag)

        @pl.when(step == 0)
        def _():
            weight_copies[2].wait()

        @pl.when(step < blocks)
        def _():
            width = query_ref.shape[1]
            wide = min(512, width)
            for start in range(0, width, wide):
                lanes = slice(start, start + wide)
                query_ref[rows_of(step), lanes] = multiply(step, query_weight, lanes)

        return carry

    lax.fori_loop(0, blocks + hops + 1, step_of, 0)

    def drain(block, carry):
        for step in range(1, across):
            y_copy(block, step).wait_send()
        for step in range(across):
            m_copy(block, step).wait_send()
        store(block).wait()
        x_copy(block).wait_send()
        for way in ways:
            for hop in range(1, hops + 1):

                @pl.when(k_due(way, hop))
                def _(way=way, hop=hop):
                    k_received(block, way, hop).wait_recv()

                @pl.when(full_sent(way, hop))
                def _(way=way, hop=hop):
                    full_copy(block, way, hop).wait_send()

                @pl.when(half_sent(way, hop))
                def _(way=way, hop=hop):
                    half_copy(block, way, hop).wait_send()

                @pl.when(k_sent(way, hop))
                def _(way=way, hop=hop):
                    k_copy(block, way, hop).wait_send()

        return carry

    lax.fori_loop(0, blocks, drain, 0)


def gather(tokens, query_weight, key_weight, value_weight):
    tp, ctx = lax.axis_size("tp"), lax.axis_size("ctx")
    across = tp // CORES
    hops = (REACH + 1) // 2
    row_count, depth = tokens.shape
    blocks = row_count // BLOCK
    query_width, key_width = query_weight.shape[1], key_weight.shape[1]
    slots = (2 * hops + 1) * 2
    dma = pltpu.SemaphoreType.DMA
    return pl.pallas_call(
        functools.partial(gather_kernel, tp, ctx, hops),
        out_shape=(
            jax.ShapeDtypeStruct((row_count, query_width), BF16),
            jax.ShapeDtypeStruct((slots, blocks, 2, BLOCK, key_width), BF16),
        ),
        in_specs=[ANY] * 4,
        out_specs=(VMEM, ANY),
        scratch_shapes=[
            pltpu.VMEM((tp, blocks, BLOCK, depth), BF16),
            pltpu.VMEM(query_weight.shape, BF16),
            pltpu.VMEM(key_weight.shape, BF16),
            pltpu.VMEM(value_weight.shape, BF16),
            pltpu.VMEM((blocks, 2, BLOCK, key_width), BF16),
            dma((blocks,)),
            dma((3,)),
            dma((blocks,)),
            dma((max(across - 1, 1), blocks)),
            dma((max(across - 1, 1), blocks)),
            dma((across, blocks)),
            dma((across, blocks)),
            dma((blocks,)),
            dma((blocks,)),
            dma((2, hops, blocks)),
            dma((2, hops, blocks)),
            dma((2, hops, blocks)),
            dma((2, hops, blocks)),
            dma((2, hops, blocks)),
            dma((2, hops, blocks)),
        ],
        compiler_params=pltpu.CompilerParams(
            collective_id=0, has_side_effects=True, vmem_limit_bytes=GRANT
        ),
        cost_estimate=pl.CostEstimate(
            flops=2 * row_count * depth * tp * (query_width + 2 * key_width),
            bytes_accessed=1 << 24,
            transcendentals=0,
        ),
    )(tokens, query_weight, key_weight, value_weight)


def finish_kernel(
    tp, chunks, wide, group, hops, links_ref, counts_ref, docs_ref, query_ref, source_ref,
    weight_ref, out_ref, source_buf, weight_buf, score_buf, attended, part_buf, own_buf,
    mate_send, mate_recv, far_send, far_recv, source_sem, weight_sems, mate_send_sems,
    mate_recv_sems, far_send_sems, far_recv_sems
):
    row_count = query_ref.shape[0]
    blocks = row_count // BLOCK
    kv_heads = source_ref.shape[3] // HEAD_DIM
    rows = row_count // tp
    tall = rows * CORES
    across = tp // CORES
    me = lax.axis_index("tp")
    chip, core = lax.div(me, CORES), lax.rem(me, CORES)
    mate = chip * CORES + 1 - core
    here = lax.axis_index("ctx")
    first = here * blocks
    anchor = (lax.div(here, 2) - hops) * 2 * blocks

    source_copy = pltpu.make_async_copy(source_ref, source_buf, source_sem.at[0])
    source_copy.start()

    def weight_copy(index):
        columns = pl.ds(pl.multiple_of(index * wide, wide), wide)
        return pltpu.make_async_copy(
            weight_ref.at[:, columns], weight_buf.at[index], weight_sems.at[index]
        )

    def start_weight(index, carry):
        weight_copy(index).start()
        return carry

    lax.fori_loop(0, chunks, start_weight, 0)

    barrier = pltpu.get_barrier_semaphore()
    pl.semaphore_signal(barrier, inc=1, device_id={"tp": mate})
    for step in range(1, across):
        other = lax.rem(chip + step, across) * CORES + core
        pl.semaphore_signal(barrier, inc=1, device_id={"tp": other})
    pl.semaphore_wait(barrier, across)
    source_copy.wait()

    scale = HEAD_DIM ** (-0.5) * 1.4426950408889634
    pair = 2 * BLOCK
    height = group * BLOCK
    token = lax.rem(lax.broadcasted_iota(jnp.int32, (height, pair), 0), BLOCK)
    column = lax.broadcasted_iota(jnp.int32, (height, pair), 1)
    row_column = lax.broadcasted_iota(jnp.int32, (1, pair), 1)

    def attend(block):
        mine = first + block
        doc = docs_ref[mine]
        live = counts_ref[block]
        places, biases = [], []
        for slot in range(LINKS):
            listed = links_ref[block, slot]
            seen = (slot < live) & ((listed <= mine) | (docs_ref[listed] != doc))
            places.append(jnp.clip(listed - anchor, 0, source_ref.shape[0] - 1))
            biases.append(jnp.where(seen, 0.0, -1e30))
        at = pl.ds(pl.multiple_of(block * BLOCK, BLOCK), BLOCK)

        def lanes_of(member):
            return slice(member * HEAD_DIM, (member + 1) * HEAD_DIM)

        def two(index, kind, head):
            return jnp.concatenate(
                [
                    source_buf[places[2 * index + i], kind, :, lanes_of(head)]
                    for i in range(2)
                ],
                axis=0,
            )

        def first_pass(query, head, index):
            scores = lax.dot_general(
                query, two(index, 0, head), (((1,), (1,)), ((), ())), preferred_element_type=F32
            )
            bias = jnp.where(row_column < BLOCK, biases[2 * index], biases[2 * index + 1])
            scores = scores + bias
            if index == 0:
                scores = jnp.where((column >= BLOCK) | (column <= token), scores, -1e30)
            score_buf[head % 2, index] = scores
            return jnp.maximum(scores[:, :BLOCK], scores[:, BLOCK:])

        def second_pass(top, head, index):
            powers = jnp.exp2(score_buf[head % 2, index] - top)
            term = jnp.dot(powers.astype(BF16), two(index, 1, head), preferred_element_type=F32)
            return powers[:, :BLOCK] + powers[:, BLOCK:], term

        top = None
        for head in range(kv_heads + 1):
            best, total, result = None, None, None
            if head < kv_heads:
                query = jnp.concatenate(
                    [query_ref[at, lanes_of(head * group + member)] for member in range(group)],
                    axis=0,
                )
                query = (query.astype(F32) * scale).astype(BF16)
            for index in range(LINKS // 2):
                if head < kv_heads:
                    both = first_pass(query, head, index)
                    best = both if best is None else jnp.maximum(best, both)
                if head > 0:
                    both, term = second_pass(top, head - 1, index)
                    total = both if total is None else total + both
                    result = term if result is None else result + term
            if head > 0:
                result = (result / jnp.sum(total, axis=1, keepdims=True)).astype(BF16)
                for member in range(group):
                    attended[at, lanes_of((head - 1) * group + member)] = result[
                        member * BLOCK : (member + 1) * BLOCK
                    ]
            if head < kv_heads:
                top = jnp.max(best, axis=1, keepdims=True)

    def mate_copy(index, step):
        return pltpu.make_async_remote_copy(
            src_ref=mate_send.at[index, step],
            dst_ref=mate_recv.at[index, step],
            send_sem=mate_send_sems.at[index, step],
            recv_sem=mate_recv_sems.at[index, step],
            device_id={"tp": mate},
        )

    def far_copy(index, step):
        other = lax.rem(chip + step, across) * CORES + core
        return pltpu.make_async_remote_copy(
            src_ref=far_send.at[index, step - 1],
            dst_ref=far_recv.at[index, step - 1],
            send_sem=far_send_sems.at[index, step - 1],
            recv_sem=far_recv_sems.at[index, step - 1],
            device_id={"tp": other},
        )

    def rows_of(which):
        return pl.ds(pl.multiple_of(which * rows, rows), rows)

    def turn_of(turn, carry):
        step = lax.rem(turn + 1, across)
        target = lax.rem(chip + step, across)
        per_chip = tall // BLOCK

        def attend_one(index, carry):
            attend(target * per_chip + index)
            return carry

        lax.fori_loop(0, per_chip, attend_one, 0)
        at = pl.ds(pl.multiple_of(target * tall, tall), tall)

        def multiply(index):
            @pl.when(turn == 0)
            def _():
                weight_copy(index).wait()

            part_buf[lax.rem(index, 2)] = jnp.dot(
                attended[at], weight_buf[index], preferred_element_type=F32
            )
            mate_send[index, step] = part_buf[lax.rem(index, 2), rows_of(1 - core)].astype(BF16)
            mate_copy(index, step).start()

        def combine(index):
            mate_copy(index, step).wait_recv()
            total = part_buf[lax.rem(index, 2), rows_of(core)] + mate_recv[index, step].astype(F32)

            @pl.when(step == 0)
            def _():
                own_buf[index] = total

            @pl.when(step > 0)
            def _():
                far_send[index, step - 1] = total.astype(BF16)
                far_copy(index, step).start()

        multiply(0)

        def middle(index, carry):
            multiply(index)
            combine(index - 1)
            return carry

        lax.fori_loop(1, chunks, middle, 0)
        combine(chunks - 1)
        return carry

    lax.fori_loop(0, across, turn_of, 0)

    def close(index, carry):
        total = own_buf[index]
        for step in range(1, across):
            far_copy(index, step).wait_recv()
            total = total + far_recv[index, step - 1].astype(F32)
        columns = pl.ds(pl.multiple_of(index * wide, wide), wide)
        out_ref[:, columns] = total.astype(BF16)
        return carry

    lax.fori_loop(0, chunks, close, 0)

    def drain(index, carry):
        for step in range(across):
            mate_copy(index, step).wait_send()
        for step in range(1, across):
            far_copy(index, step).wait_send()
        return carry

    lax.fori_loop(0, chunks, drain, 0)


def finish(links, counts, doc_ids, query, source, out_weight):
    tp = lax.axis_size("tp")
    across = tp // CORES
    hops = (REACH + 1) // 2
    row_count, depth = query.shape
    width = out_weight.shape[1]
    group = depth // source.shape[3]
    rows = row_count // tp
    wide = min(512, width)
    chunks = width // wide
    dma = pltpu.SemaphoreType.DMA
    return pl.pallas_call(
        functools.partial(finish_kernel, tp, chunks, wide, group, hops),
        out_shape=jax.ShapeDtypeStruct((rows, width), BF16),
        in_specs=[SMEM, SMEM, SMEM, VMEM, ANY, ANY],
        out_specs=VMEM,
        scratch_shapes=[
            pltpu.VMEM(source.shape, BF16),
            pltpu.VMEM((chunks, depth, wide), BF16),
            pltpu.VMEM((2, LINKS // 2, group * BLOCK, 2 * BLOCK), F32),
            pltpu.VMEM((row_count, depth), BF16),
            pltpu.VMEM((2, rows * CORES, wide), F32),
            pltpu.VMEM((chunks, rows, wide), F32),
            pltpu.VMEM((chunks, across, rows, wide), BF16),
            pltpu.VMEM((chunks, across, rows, wide), BF16),
            pltpu.VMEM((chunks, max(across - 1, 1), rows, wide), BF16),
            pltpu.VMEM((chunks, max(across - 1, 1), rows, wide), BF16),
            dma((1,)),
            dma((chunks,)),
            dma((chunks, across)),
            dma((chunks, across)),
            dma((chunks, max(across - 1, 1))),
            dma((chunks, max(across - 1, 1))),
        ],
        compiler_params=pltpu.CompilerParams(
            collective_id=1, has_side_effects=True, vmem_limit_bytes=GRANT
        ),
        cost_estimate=pl.CostEstimate(
            flops=2 * row_count * depth * (width + 2 * LINKS * BLOCK),
            bytes_accessed=1 << 24,
            transcendentals=0,
        ),
    )(links, counts, doc_ids, query, source, out_weight)


def local(tokens, query_weight, key_weight, value_weight, out_weight, links, counts, doc_ids):
    query, source = gather(tokens, query_weight, key_weight, value_weight)
    source = source.reshape((-1,) + source.shape[2:])
    return finish(links, counts, doc_ids, query, source, out_weight)


def solution(mesh):
    placed = (
        P("ctx", "tp"),
        P(None, "tp"),
        P(None, "tp"),
        P(None, "tp"),
        P("tp", None),
        P("ctx", None),
        P("ctx"),
        P(),
    )
    return jax.shard_map(
        local, mesh=mesh, in_specs=placed, out_specs=P(("ctx", "tp"), None), check_vma=False
    )
```
